128 devices in a mesh: dp: 8 (over x, core), ctx: 16 (over z, y).
Axes of the slice: x: 4, y: 4, z: 4, core: 2. Of those that a mesh axis runs over, the one named last changes fastest.
Arguments:
- layer_input: bfloat16 [8, 4096, 2048], P('dp', 'ctx'), may hold values from -6 to 6
- queries: bfloat16 [8, 4096, 1024], P('dp', 'ctx'), may hold values from -6 to 6
- gates: float32 [8, 4096, 8], P('dp', 'ctx'), may hold values from 0 to 1
- regularizer: float32 [8], replicated, may hold values from 0.25 to 1
- key_weight: bfloat16 [2048, 1024], replicated, may hold values from -0.0234375 to 0.0234375
- value_weight: bfloat16 [2048, 1024], replicated, may hold values from -0.125 to 0.125
- out_cotangent: bfloat16 [8, 4096, 1024], P('dp', 'ctx'), may hold values from -6 to 6
- lengths: int32 [8, 16], P('dp', 'ctx'), may hold values from 0 to 256, as said below
Outputs:
- input_grad: bfloat16 [8, 4096, 2048], P('dp', 'ctx')
- query_grad: float32 [8, 4096, 1024], P('dp', 'ctx')
- key_weight_grad: float32 [2048, 1024], P(('dp', 'ctx'))
- value_weight_grad: float32 [2048, 1024], P(('dp', 'ctx'))
The draws below stay inside these ranges and needn't reach their ends.
Inputs may be any that keep to these rules, and one draw needn't show every extreme that they name: lengths[s, c] counts the valid tokens of block c of sequence s; the valid tokens of a sequence are its first ones, and at least half of 4096.
All inputs are finite; a program needn't handle non-finite values.
Results may differ from the reference program's by a relative error of at most 0.005.
Values sent between devices are 32-bit elements; how exact they have to be, the bound alone decides.
A program may use at most 128 MiB of HBM per device.

```python
import math
import jax
import jax.numpy as jnp
from jax import lax

D = 2048
HEAD_COUNT = 8
DK = 128
ITERS = 4
BLOCK_TOKENS = 256
SEQUENCE_COUNT = 8
BLOCK_COUNT = 16
SEQ_LEN = 4096


def draw_gates(key, part):
    key = jax.random.fold_in(key, 11)
    key_collection = jax.random.split(key, 7)
    sequence_length = BLOCK_TOKENS * BLOCK_COUNT
    slow_share = 0.5
    slow_pick = jax.random.uniform(key_collection[0], (SEQUENCE_COUNT, 1, 1, HEAD_COUNT)) < slow_share
    slow_rate = jnp.exp(jax.random.uniform(key_collection[1], (SEQUENCE_COUNT, 1, 1, HEAD_COUNT), jnp.float32, math.log(0.05), math.log(0.5))) / sequence_length
    fast_rate = jnp.exp(jax.random.uniform(key_collection[2], (SEQUENCE_COUNT, 1, 1, HEAD_COUNT), jnp.float32, math.log(1.0 / 50.0), math.log(1.0 / 30.0)))
    rate_per_head = jnp.where(slow_pick, slow_rate, fast_rate)
    scale_per_block = jnp.exp(jax.random.uniform(key_collection[3], (SEQUENCE_COUNT, BLOCK_COUNT, 1, HEAD_COUNT), jnp.float32, math.log(0.5), math.log(2.0)))
    coarse_scale = jnp.exp(jax.random.uniform(key_collection[4], (SEQUENCE_COUNT, BLOCK_COUNT, BLOCK_TOKENS, HEAD_COUNT), jnp.float32, math.log(0.5), math.log(2.0)))
    spike_mask = jax.random.uniform(key_collection[5], (SEQUENCE_COUNT, BLOCK_COUNT, BLOCK_TOKENS, HEAD_COUNT)) < 3.0 / sequence_length
    spike_keep_mask = jax.random.uniform(key_collection[6], (SEQUENCE_COUNT, BLOCK_COUNT, BLOCK_TOKENS, HEAD_COUNT), jnp.float32, 0.5, 0.8)
    gate_logarithm = -rate_per_head * scale_per_block * coarse_scale + jnp.where(spike_mask, jnp.log(spike_keep_mask), 0.0)
    return jnp.exp(gate_logarithm).reshape(SEQUENCE_COUNT, sequence_length, HEAD_COUNT).astype(jnp.float32)


def draw_lengths(key, part):
    key = jax.random.fold_in(key, 7)
    sequence_length = BLOCK_TOKENS * BLOCK_COUNT
    seq_total = jax.random.randint(key, (SEQUENCE_COUNT, 1), sequence_length // 2, sequence_length + 1)
    starts = jnp.arange(BLOCK_COUNT, dtype=jnp.int32)[None, :] * BLOCK_TOKENS
    return jnp.clip(seq_total - starts, 0, BLOCK_TOKENS).astype(jnp.int32)


def block_scale(stream_key, extent, shards, low, high):
    level = 1.0
    for dim, blocks in shards:
        heights = jax.random.uniform(jax.random.fold_in(jax.random.fold_in(stream_key, 6), dim), (blocks,), jnp.float32, low / len(shards), high / len(shards))
        level = level * jnp.repeat(jnp.exp(heights), extent[dim] // blocks).reshape((-1,) + (1,) * (len(extent) - 1 - dim))
    return level


def centred(rng, shape, spread, most, shards=(), kind=jnp.bfloat16):
    entries = spread * jax.random.normal(rng, shape, jnp.float32)
    if shards:
        entries = entries * block_scale(rng, shape, shards, -0.22, 0.18)
    return jnp.clip(entries, -most, most).astype(kind)


def setup_inputs(seed: int = 0) -> dict:
    arg_keys = jax.random.split(jax.random.key(seed), 9)
    layer_input = centred(arg_keys[0], (SEQUENCE_COUNT, SEQ_LEN, D), 1.0, 6.0, ((0, 8), (1, 16)))
    queries = centred(arg_keys[1], (SEQUENCE_COUNT, SEQ_LEN, HEAD_COUNT * DK), 1.0, 6.0, ((0, 8), (1, 16)))
    gates = draw_gates(jax.random.fold_in(arg_keys[8], 71), 0)
    regularizer = jnp.clip(jnp.exp(jax.random.uniform(arg_keys[3], (HEAD_COUNT,), jnp.float32, math.log(0.25), math.log(1.0))), 0.25, 1.0)
    key_weight = centred(arg_keys[4], (D, HEAD_COUNT * DK), (D * DK // 4) ** -0.5, 0.0234375)
    value_weight = centred(arg_keys[5], (D, HEAD_COUNT * DK), D ** -0.5, 0.125)
    out_cotangent = centred(arg_keys[6], (SEQUENCE_COUNT, SEQ_LEN, HEAD_COUNT * DK), 1.0, 6.0, ((0, 8), (1, 16)))
    lengths = draw_lengths(jax.random.fold_in(arg_keys[8], 71), 0)
    return {"layer_input": layer_input, "queries": queries, "gates": gates, "regularizer": regularizer, "key_weight": key_weight, "value_weight": value_weight, "out_cotangent": out_cotangent, "lengths": lengths}


HIGHEST = lax.Precision.HIGHEST
tiny = 1e-06

def contract(form, *operands):
    return jnp.einsum(form, *operands, precision=HIGHEST)

def decay_tables(gate_logarithm):
    running = jnp.cumsum(gate_logarithm, axis=0)
    heads_first = running.T
    log_gap = heads_first[:, :, None] - heads_first[:, None, :]
    tokens_len = gate_logarithm.shape[0]
    causal = jnp.arange(tokens_len)[:, None] >= jnp.arange(tokens_len)[None, :]
    decay_table = jnp.exp(jnp.where(causal[None], log_gap, -1e+30))
    return (decay_table, jnp.exp(running), jnp.exp(running[-1:] - running), running[-1])

def apply_system(operand, key_rows, decay_table, start_w, key_gram, ridge):
    scores = contract('thd,shd->hts', operand, key_rows) * decay_table
    inner_part = contract('hts,shd->thd', scores, key_rows)
    outer_part = start_w[:, :, None] * contract('thd,hde->the', operand, key_gram)
    return ridge[None, :, None] * operand + outer_part + inner_part

def conj_grad(right_side, key_rows, decay_table, start_w, key_gram, ridge):
    solution = jnp.zeros_like(right_side)
    residual = right_side
    direction = right_side
    norm_now = lax.optimization_barrier(jnp.sum(residual * residual, axis=-1))
    for iteration in range(ITERS):
        image_vec = apply_system(direction, key_rows, decay_table, start_w, key_gram, ridge)
        step_size = norm_now / (lax.optimization_barrier(jnp.sum(direction * image_vec, axis=-1)) + tiny)
        solution = solution + step_size[..., None] * direction
        residual = residual - step_size[..., None] * image_vec
        norm_next = lax.optimization_barrier(jnp.sum(residual * residual, axis=-1))
        direction = residual + (norm_next / (norm_now + tiny))[..., None] * direction
        norm_now = norm_next
    return solution

def block_solves(key_rows, value_rows, query_rows, cot_rows, decay_table, start_w, key_gram, value_key, ridge):
    solution = conj_grad(query_rows, key_rows, decay_table, start_w, key_gram, ridge)
    value_scores = contract('thv,shv->hts', cot_rows, value_rows) * decay_table
    right_side = start_w[:, :, None] * contract('thv,hvd->thd', cot_rows, value_key)
    right_side = right_side + contract('hts,shd->thd', value_scores, key_rows)
    adjoint = conj_grad(right_side, key_rows, decay_table, start_w, key_gram, ridge)
    return (solution, adjoint, value_scores)

def local_states(key_rows, value_rows, end_w):
    return (contract('sh,shd,she->hde', end_w, key_rows, key_rows), contract('sh,shv,shd->hvd', end_w, value_rows, key_rows))

def back_states(solution, adjoint, cot_rows, start_w):
    cross = contract('th,thd,the->hde', start_w, adjoint, solution)
    return (-(cross + jnp.swapaxes(cross, 1, 2)), contract('th,thv,thd->hvd', start_w, cot_rows, solution))

def block_grads(key_rows, value_rows, solution, adjoint, cot_rows, value_scores, decay_table, end_w, sym_back, pair_back):
    sol_scores = contract('thd,shd->hts', solution, key_rows) * decay_table
    adj_scores = contract('thd,shd->hts', adjoint, key_rows) * decay_table
    key_grad = contract('hts,thd->shd', value_scores, solution)
    key_grad = key_grad - contract('hts,thd->shd', sol_scores, adjoint)
    key_grad = key_grad - contract('hts,thd->shd', adj_scores, solution)
    carried = contract('shd,hde->she', key_rows, sym_back) + contract('shv,hvd->shd', value_rows, pair_back)
    key_grad = key_grad + end_w[:, :, None] * carried
    value_grad = contract('hts,thv->shv', sol_scores, cot_rows)
    value_grad = value_grad + end_w[:, :, None] * contract('shd,hvd->shv', key_rows, pair_back)
    return (key_grad, value_grad)

def prepare(block_input, block_queries, block_gates, block_cot, length, key_weight, value_weight):
    tokens_len = block_input.shape[0]
    heads = block_gates.shape[1]
    valid_mask = (jnp.arange(tokens_len, dtype=jnp.int32) < length).astype(jnp.float32)[:, None, None]
    key_rows = jnp.dot(block_input, key_weight, preferred_element_type=jnp.float32).reshape(tokens_len, heads, -1) * valid_mask
    value_rows = jnp.dot(block_input, value_weight, preferred_element_type=jnp.float32).reshape(tokens_len, heads, -1) * valid_mask
    query_rows = block_queries.astype(jnp.float32).reshape(tokens_len, heads, -1)
    cot_rows = block_cot.astype(jnp.float32).reshape(tokens_len, heads, -1) * valid_mask
    return (valid_mask, key_rows, value_rows, query_rows, cot_rows)

def one_sequence(seq_input, seq_queries, seq_gates, seq_cot, seq_lengths, key_weight, value_weight, regularizer):

    def by_block(array):
        return array.reshape((BLOCK_COUNT, BLOCK_TOKENS) + array.shape[1:])
    inputs = (by_block(seq_input), by_block(seq_queries), by_block(seq_gates), by_block(seq_cot), seq_lengths)
    empty_state = jnp.zeros((HEAD_COUNT, DK, DK), jnp.float32)

    def forward(partial_value, block_item):
        key_gram, value_key = partial_value
        block_input, block_queries, block_gates, block_cot, length = block_item
        valid_mask, key_rows, value_rows, query_rows, cot_rows = prepare(block_input, block_queries, block_gates, block_cot, length, key_weight, value_weight)
        decay_table, start_w, end_w, block_total = decay_tables(jnp.log(block_gates))
        solution, adjoint, value_scores = block_solves(key_rows, value_rows, query_rows, cot_rows, decay_table, start_w, key_gram, value_key, regularizer)
        gram_local, pair_local = local_states(key_rows, value_rows, end_w)
        factor = jnp.exp(block_total)[:, None, None]
        return ((factor * key_gram + gram_local, factor * value_key + pair_local), (solution, adjoint))
    _, (solutions, adjoints) = lax.scan(forward, (empty_state, empty_state), inputs)

    def backward(partial_value, block_item):
        sym_back, pair_back = partial_value
        block_input, block_queries, block_gates, block_cot, length, solution, adjoint = block_item
        valid_mask, key_rows, value_rows, query_rows, cot_rows = prepare(block_input, block_queries, block_gates, block_cot, length, key_weight, value_weight)
        decay_table, start_w, end_w, block_total = decay_tables(jnp.log(block_gates))
        value_scores = contract('thv,shv->hts', cot_rows, value_rows) * decay_table
        key_grad, value_grad = block_grads(key_rows, value_rows, solution, adjoint, cot_rows, value_scores, decay_table, end_w, sym_back, pair_back)
        sym_local, pair_local = back_states(solution, adjoint, cot_rows, start_w)
        factor = jnp.exp(block_total)[:, None, None]
        return ((factor * sym_back + sym_local, factor * pair_back + pair_local), (key_grad * valid_mask, value_grad * valid_mask))
    _, (key_grads, value_grads) = lax.scan(backward, (empty_state, empty_state), inputs + (solutions, adjoints), reverse=True)
    key_flat = key_grads.reshape(SEQ_LEN, HEAD_COUNT * DK).astype(jnp.bfloat16)
    value_flat = value_grads.reshape(SEQ_LEN, HEAD_COUNT * DK).astype(jnp.bfloat16)
    dims = (((1,), (1,)), ((), ()))
    input_grad = lax.dot_general(key_flat, key_weight, dims, preferred_element_type=jnp.float32)
    input_grad = input_grad + lax.dot_general(value_flat, value_weight, dims, preferred_element_type=jnp.float32)
    rows_dims = (((0,), (0,)), ((), ()))
    key_wgrad = lax.dot_general(seq_input, key_flat, rows_dims, preferred_element_type=jnp.float32)
    value_wgrad = lax.dot_general(seq_input, value_flat, rows_dims, preferred_element_type=jnp.float32)
    return (input_grad.astype(jnp.bfloat16), adjoints.reshape(SEQ_LEN, HEAD_COUNT * DK), key_wgrad, value_wgrad)

def reference(layer_input, queries, gates, regularizer, key_weight, value_weight, out_cotangent, lengths):
    model_width = layer_input.shape[2]

    def per_sequence(totals, seq_item):
        input_part, query_part, key_wgrad, value_wgrad = one_sequence(*seq_item, key_weight, value_weight, regularizer)
        return ((totals[0] + key_wgrad, totals[1] + value_wgrad), (input_part, query_part))
    empty_grad = jnp.zeros((model_width, HEAD_COUNT * DK), jnp.float32)
    (key_total, value_total), (input_grad, query_grad) = lax.scan(per_sequence, (empty_grad, empty_grad), (layer_input, queries, gates, out_cotangent, lengths))
    return (input_grad, query_grad, key_total, value_total)
```

```python
import functools

import jax
import jax.numpy as jnp
from jax import lax
from jax.experimental import pallas as pl
from jax.experimental.pallas import tpu as pltpu
from jax.sharding import PartitionSpec as P

ITERS = 4
TINY = 1e-06
DK = 128
PAIR = 2
F32 = jnp.float32
BF16 = jnp.bfloat16
MESH = pl.DeviceIdType.MESH


def split(a):
    high = a.astype(BF16)
    return high, (a - high.astype(F32)).astype(BF16)


def dot(a, b):
    return jnp.dot(a, b, preferred_element_type=F32)


def left3(parts):
    high, low = parts
    return jnp.concatenate([high, low, high], axis=1)


def right3(parts):
    high, low = parts
    return jnp.concatenate([high, high, low], axis=0)


def dot3(a, b):
    return dot(left3(a), right3(b))


def mesa_kernel(
    sizes,
    x_ref, q_ref, gates_ref, reg_ref, wk_ref, wv_ref, g_ref, len_ref,
    ig_ref, qg_ref, kwg_ref, vwg_ref,
    x_s, w_s, q_s, g_s, gate_s, run_s, tot_s, sw_s, ew_s, fac_snd, fac_rcv,
    kv_s, kt_s, dt_s, vs_s, rhs_s, ewc_s, loc_s,
    snd1, rcv1, rcv2, snd3, rcv3, rcv4,
    xs_snd, xs_rcv, xt_s, gr_s, sib_snd, sib_rcv, wp_s,
    ra1, ra2, ra3, rb1, rb2, rb3, rc1, rc2, rc3,
    ld_sem, w_sem, fac_sem, x_sem, sib_sem, s1, r1, s2, r2, s3, r3, s4, r4, rs_snd, rs_rcv,
):
    nx, nz, ny, heads, tokens, width = sizes
    nctx = nz * ny
    groups = heads // PAIR
    srows = DK // nctx
    xb = width // (2 * nx)
    rows = xb // nctx
    half = rows // 2
    dp, ctx = lax.axis_index("dp"), lax.axis_index("ctx")
    mx, mc = lax.div(dp, 2), lax.rem(dp, 2)
    mz, my = lax.div(ctx, ny), lax.rem(ctx, ny)
    sib = mx * 2 + (1 - mc)

    barrier = pltpu.get_barrier_semaphore()
    for o in range(1, nctx):
        pl.semaphore_signal(barrier, inc=1, device_id=(dp, lax.rem(ctx + o, nctx)), device_id_type=MESH)
    pl.semaphore_signal(barrier, inc=1, device_id=(sib, ctx), device_id_type=MESH)
    for o in range(1, nx):
        pl.semaphore_signal(
            barrier, inc=1, device_id=(lax.rem(mx + o, nx) * 2 + mc, ctx), device_id_type=MESH
        )

    pltpu.make_async_copy(x_ref.at[0], x_s, ld_sem.at[0]).start()
    for h in range(heads):
        cols = pl.ds(h * DK, DK)
        pltpu.make_async_copy(wk_ref.at[:, cols], w_s.at[h, :, pl.ds(0, DK)], w_sem.at[h]).start()
        pltpu.make_async_copy(wv_ref.at[:, cols], w_s.at[h, :, pl.ds(DK, DK)], w_sem.at[h]).start()
    for h in range(heads):
        cols = pl.ds(h * DK, DK)
        pltpu.make_async_copy(g_ref.at[0, :, cols], g_s.at[h], ld_sem.at[1]).start()
        pltpu.make_async_copy(q_ref.at[0, :, cols], q_s.at[h], ld_sem.at[2]).start()

    length = len_ref[0, 0]
    gate_s[...] = jnp.ones_like(gate_s)
    gate_s[:, 0:heads] = gates_ref[0]
    run = jnp.log(gate_s[...].T[0:heads])
    lane = lax.broadcasted_iota(jnp.int32, (heads, tokens), 1)
    step = 1
    while step < tokens:
        run = run + jnp.where(lane >= step, pltpu.roll(run, step, 1), 0.0)
        step *= 2
    total = jnp.broadcast_to(run[:, tokens - 1 : tokens], (heads, tokens))
    run_s[...] = run
    tot_s[...] = total
    sw_s[...] = jnp.exp(run)
    ew_s[...] = jnp.exp(total - run)
    fac_snd[...] = jnp.exp(total)

    mask_rows = (lax.broadcasted_iota(jnp.int32, (tokens, 2 * DK), 0) < length).astype(F32)
    mask_lane = (lax.broadcasted_iota(jnp.int32, (1, tokens), 1) < length).astype(F32)

    def all_to_all(src, dst, g, send, recv):
        for o in range(1, nctx):
            to = lax.rem(ctx + o, nctx)
            pltpu.make_async_remote_copy(
                src_ref=src.at[g, to], dst_ref=dst.at[g, ctx], send_sem=send.at[g], recv_sem=recv.at[g],
                device_id=(dp, to), device_id_type=MESH,
            ).start()
        pltpu.make_async_copy(src.at[g, ctx], dst.at[g, ctx], recv.at[g]).start()

    def wait_all(buf, sem):
        pltpu.make_async_copy(buf, buf, sem).wait()

    def wait_sent(buf, g, sem):
        part = buf.at[g, pl.ds(0, nctx - 1)]
        pltpu.make_async_copy(part, part, sem.at[g]).wait()

    def project(g):
        for i in range(PAIR):
            h = g * PAIR + i
            wait_all(w_s.at[h], w_sem.at[h])
            kv = dot(x_s[...], w_s[h]) * mask_rows
            parts = split(kv)
            kv_s[h, 0], kv_s[h, 1] = parts
            kt = kv[:, 0:DK].T
            kt_s[h, 0], kt_s[h, 1] = split(kt)
            state = dot3(split(kt * ew_s[pl.ds(h, 1), :]), parts)
            snd1[g, :, i] = state.reshape(nctx, srows, 2 * DK)

    def tables(g):
        for i in range(PAIR):
            h = g * PAIR + i
            run_row = run_s[pl.ds(h, 1), :]
            run_col = jnp.broadcast_to(run_row, (DK, tokens)).T
            ewc_s[h] = jnp.exp(tot_s[pl.ds(h, 1), :][:, 0:DK] - run_col)
            gap = run_row - jnp.concatenate([run_col] * (tokens // DK), axis=1)
            later = lax.broadcasted_iota(jnp.int32, (tokens, tokens), 1) >= lax.broadcasted_iota(
                jnp.int32, (tokens, tokens), 0
            )
            table = jnp.exp(jnp.where(later, gap, -1e30))
            dt_s[h] = table
            gt = ((g_s[h].astype(F32)).T * mask_lane).astype(BF16)
            v_both = jnp.concatenate([kv_s[h, 0, :, DK:], kv_s[h, 1, :, DK:]], axis=1)
            scores = dot(v_both, jnp.concatenate([gt, gt], axis=0)) * table
            vs_s[h] = scores
            rhs_s[h] = dot3((kt_s[h, 0], kt_s[h, 1]), split(scores))

    def prefix(buf, g, order):
        held = [jnp.zeros((srows, 2 * DK), F32) for _ in range(PAIR)]
        for c in order:
            for i in range(PAIR):
                mine = buf[g, c, i]
                buf[g, c, i] = held[i]
                held[i] = fac_rcv[c, pl.ds(g * PAIR + i, 1), :] * held[i] + mine

    def solve(g):
        state = [rcv2[g, :, i].reshape(DK, 2 * DK) for i in range(PAIR)]
        x, r, p, rr, keys, kts, big, gts = ([None] * PAIR for _ in range(8))
        for i in range(PAIR):
            h = g * PAIR + i
            qt = q_s[h].astype(F32).T
            gts[i] = ((g_s[h].astype(F32)).T * mask_lane).astype(BF16)
            gram, pair = split(state[i][:, 0:DK]), split(state[i][:, DK:])
            right = rhs_s[h] + sw_s[pl.ds(h, 1), :] * dot(
                jnp.concatenate(pair, axis=1), jnp.concatenate([gts[i], gts[i]], axis=0)
            )
            p[i] = r[i] = jnp.concatenate([qt, right], axis=1)
            rr[i] = jnp.sum(r[i] * r[i], axis=0, keepdims=True)
            keys[i] = (kv_s[h, 0, :, 0:DK], kv_s[h, 1, :, 0:DK])
            kts[i] = (kt_s[h, 0], kt_s[h, 1])
            big[i] = tuple(jnp.concatenate([a, b], axis=0) for a, b in zip(keys[i], gram))
        for it in range(ITERS):
            last = it == ITERS - 1
            for i in range(PAIR):
                h = g * PAIR + i
                table = jnp.concatenate([dt_s[h]] * 2, axis=1)
                sw = jnp.concatenate([sw_s[pl.ds(h, 1), :]] * 2, axis=1)
                if last:
                    both = dot(big[i][0], p[i].astype(BF16))
                    inner = dot(kts[i][0], (both[0:tokens] * table).astype(BF16))
                else:
                    both = dot3(big[i], split(p[i]))
                    inner = dot3(kts[i], split(both[0:tokens] * table))
                image = reg_ref[h] * p[i] + sw * both[tokens:] + inner
                size = rr[i] / (jnp.sum(p[i] * image, axis=0, keepdims=True) + TINY)
                x[i] = size * p[i] if it == 0 else x[i] + size * p[i]
                if not last:
                    r[i] = r[i] - size * image
                    following = jnp.sum(r[i] * r[i], axis=0, keepdims=True)
                    p[i] = r[i] + (following / (rr[i] + TINY)) * p[i]
                    rr[i] = following
        for i in range(PAIR):
            h = g * PAIR + i
            xt, yt = x[i][:, 0:tokens], x[i][:, tokens:]
            xn, yn = xt.T, yt.T
            qg_ref[0, :, pl.ds(pl.multiple_of(h * DK, DK), DK)] = yn
            gn = (g_s[h].astype(F32) * mask_rows[:, 0:DK]).astype(BF16)
            y_high, y_low = split(yn)
            yg = (
                jnp.concatenate([y_high, gn], axis=1),
                jnp.concatenate([y_low, jnp.zeros_like(gn)], axis=1),
            )
            back = dot3(split(xt * sw_s[pl.ds(h, 1), :]), yg)
            snd3[g, :, i] = back.reshape(nctx, srows, 2 * DK)
            table = jnp.concatenate([dt_s[h]] * 2, axis=1)
            scores = dot3(keys[i], split(x[i])) * table
            sol, adj = scores[:, 0:tokens], scores[:, tokens:]
            from_x = dot3(split(vs_s[h] - adj), split(xn))
            from_yg = dot3(split(sol), yg)
            loc_s[h] = jnp.concatenate([from_x - from_yg[:, 0:DK], from_yg[:, DK:]], axis=1)

    def gradients(g):
        for i in range(PAIR):
            h = g * PAIR + i
            state = rcv4[g, :, i].reshape(DK, 2 * DK)
            cross, pair_t = state[:, 0:DK], state[:, DK:]
            sym, pair = -(cross + cross.T), pair_t.T
            both = jnp.concatenate(
                [
                    jnp.concatenate([sym, pair_t], axis=1),
                    jnp.concatenate([pair, jnp.zeros_like(pair)], axis=1),
                ],
                axis=0,
            )
            carried = dot3((kv_s[h, 0], kv_s[h, 1]), split(both))
            decay = jnp.concatenate([ewc_s[h]] * 2, axis=1)
            grad = ((loc_s[h] + decay * carried) * mask_rows).astype(BF16)
            gr_s[g, 0:tokens, pl.ds(i * 2 * DK, 2 * DK)] = grad
            sib_snd[g, :, pl.ds(i * 2 * DK, 2 * DK)] = grad.astype(F32)

    def sib_copy(g):
        return pltpu.make_async_remote_copy(
            src_ref=sib_snd.at[g], dst_ref=sib_rcv.at[g], send_sem=sib_sem.at[0, g], recv_sem=sib_sem.at[1, g],
            device_id=(sib, ctx), device_id_type=MESH,
        )

    me = {"x": mx, "z": mz, "y": my}
    count = {"x": nx, "z": nz, "y": ny}
    lanes3, lanes1 = pl.ds(0, 3 * DK), pl.ds(3 * DK, DK)
    parts = (
        ("xyz", pl.ds(0, half), lanes3, (ra1, ra2, ra3)),
        ("yzx", pl.ds(half, half), lanes3, (rb1, rb2, rb3)),
        ("zxy", pl.ds(0, rows), lanes1, (rc1, rc2, rc3)),
    )

    def device(axis, at):
        place = dict(me)
        place[axis] = at
        return (place["x"] * 2 + mc, place["z"] * ny + place["y"])

    def chunk(n, part, g, at):
        order, rws, lns, bufs = parts[part]
        left = [a for a in "xzy" if a not in order[:n]]
        spot = tuple(at if a == order[n] else slice(None) for a in left)
        if n == 0:
            return wp_s.at[(g,) + spot + (rws, lns)]
        return bufs[n - 1].at[(g, 0) + spot]

    def scatter_start(n, g):
        for part, (order, rws, lns, bufs) in enumerate(parts):
            axis = order[n]
            for o in range(1, count[axis]):
                to = lax.rem(me[axis] + o, count[axis])
                pltpu.make_async_remote_copy(
                    src_ref=chunk(n, part, g, to), dst_ref=bufs[n].at[g, o - 1],
                    send_sem=rs_snd.at[part, n, g], recv_sem=rs_rcv.at[part, n, g],
                    device_id=device(axis, to), device_id_type=MESH,
                ).start()

    def scatter_add(n, g):
        for part, (order, rws, lns, bufs) in enumerate(parts):
            wait_all(bufs[n].at[g], rs_rcv.at[part, n, g])
            summed = chunk(n, part, g, me[order[n]])[...]
            for o in range(count[order[n]] - 1):
                summed = summed + bufs[n][g, o]
            if n < 2:
                bufs[n][g, 0] = summed
            else:
                first = pl.ds(pl.multiple_of(g * PAIR * DK, DK), DK)
                second = pl.ds(pl.multiple_of(g * PAIR * DK + DK, DK), DK)
                if part < 2:
                    kwg_ref[rws, first] = summed[:, 0:DK]
                    vwg_ref[rws, first] = summed[:, DK : 2 * DK]
                    kwg_ref[rws, second] = summed[:, 2 * DK :]
                else:
                    vwg_ref[rws, second] = summed

    def weight_part(g):
        sib_copy(g).wait_recv()
        gr_s[g, tokens:, :] = sib_rcv[g].astype(BF16)
        for k in range(nx):
            out = dot(xt_s[k * xb : (k + 1) * xb, :], gr_s[g])
            wp_s[g, k] = out.reshape(nz, ny, rows, PAIR * 2 * DK)
        scatter_start(0, g)

    def input_gradient():
        def columns(n, carry):
            span = pl.ds(pl.multiple_of(n * 256, 256), 256)
            total = None
            for h in range(heads):
                grad = gr_s[h // PAIR, 0:tokens, (h % PAIR) * 2 * DK : (h % PAIR + 1) * 2 * DK]
                term = lax.dot_general(
                    grad, w_s[h, span, :], (((1,), (1,)), ((), ())), preferred_element_type=F32
                )
                total = term if total is None else total + term
            ig_ref[0, :, span] = total.astype(BF16)
            return carry

        lax.fori_loop(0, width // 256, columns, 0)

    wait_all(x_s, ld_sem.at[0])
    project(0)
    pl.semaphore_wait(barrier, nctx - 1 + 1 + nx - 1)
    for o in range(1, nctx):
        to = lax.rem(ctx + o, nctx)
        pltpu.make_async_remote_copy(
            src_ref=fac_snd, dst_ref=fac_rcv.at[ctx], send_sem=fac_sem.at[0], recv_sem=fac_sem.at[1],
            device_id=(dp, to), device_id_type=MESH,
        ).start()
    pltpu.make_async_copy(fac_snd, fac_rcv.at[ctx], fac_sem.at[1]).start()
    all_to_all(snd1, rcv1, 0, s1, r1)

    def project_next(g, carry):
        project(g)
        all_to_all(snd1, rcv1, g, s1, r1)
        return carry

    lax.fori_loop(1, groups, project_next, 0)

    for k in range(nx):
        theirs = pl.ds(pl.multiple_of(k * 2 * xb + (1 - mc) * xb, xb), xb)
        xs_snd[:, k * xb : (k + 1) * xb] = x_s[:, theirs].astype(F32)
    x_copy = pltpu.make_async_remote_copy(
        src_ref=xs_snd, dst_ref=xs_rcv, send_sem=x_sem.at[0], recv_sem=x_sem.at[1],
        device_id=(sib, ctx), device_id_type=MESH,
    )
    x_copy.start()
    wait_all(g_s, ld_sem.at[1])
    wait_all(q_s, ld_sem.at[2])

    def tables_next(g, carry):
        tables(g)
        return carry

    lax.fori_loop(0, groups, tables_next, 0)
    for k in range(nx):
        mine = pl.ds(pl.multiple_of(k * 2 * xb + mc * xb, xb), xb)
        xt_s[k * xb : (k + 1) * xb, 0:tokens] = x_s[:, mine].astype(F32).T.astype(BF16)
    x_copy.wait_recv()
    for k in range(nx):
        xt_s[k * xb : (k + 1) * xb, tokens:] = xs_rcv[:, k * xb : (k + 1) * xb].T.astype(BF16)
    wait_all(fac_rcv, fac_sem.at[1])

    def during(s, first, fn):
        @pl.when(jnp.logical_and(s >= first, s < first + groups))
        def _():
            fn(s - first)

    def forward_prefix(g):
        wait_all(rcv1.at[g], r1.at[g])
        prefix(rcv1, g, range(nctx))
        all_to_all(rcv1, rcv2, g, s2, r2)

    def solves(g):
        wait_all(rcv2.at[g], r2.at[g])
        solve(g)
        all_to_all(snd3, rcv3, g, s3, r3)

    def backward_grads(g):
        wait_all(rcv4.at[g], r4.at[g])
        gradients(g)
        sib_copy(g).start()

    def backward_prefix(g):
        wait_all(rcv3.at[g], r3.at[g])
        prefix(rcv3, g, range(nctx - 1, -1, -1))
        all_to_all(rcv3, rcv4, g, s4, r4)

    def reduce_two(g):
        scatter_add(0, g)
        scatter_start(1, g)

    def reduce_three(g):
        scatter_add(1, g)
        scatter_start(2, g)

    def reduce_last(g):
        scatter_add(2, g)

    def one(s, carry):
        during(s, 0, forward_prefix)
        during(s, 1, solves)
        during(s, 3, backward_grads)
        during(s, 2, backward_prefix)
        during(s, 3, weight_part)
        pl.when(s == groups + 3)(input_gradient)
        during(s, 6, reduce_last)
        during(s, 5, reduce_three)
        during(s, 4, reduce_two)
        return carry

    lax.fori_loop(0, groups + 6, one, 0)

    sent = pltpu.make_async_copy(
        fac_rcv.at[pl.ds(0, nctx - 1)], fac_rcv.at[pl.ds(0, nctx - 1)], fac_sem.at[0]
    )
    sent.wait()
    x_copy.wait_send()

    def drain(g, carry):
        wait_sent(snd1, g, s1)
        wait_sent(rcv1, g, s2)
        wait_sent(snd3, g, s3)
        wait_sent(rcv3, g, s4)
        sib_copy(g).wait_send()
        for part in range(3):
            for n in range(3):
                buf = parts[part][3][n].at[g]
                wait_all(buf, rs_snd.at[part, n, g])
        return carry

    lax.fori_loop(0, groups, drain, 0)


def solution(mesh):
    nx = mesh.shape["dp"] // 2
    nctx = mesh.shape["ctx"]
    nz = ny = {16: 4, 4: 2}[nctx]

    def body(layer_input, queries, gates, regularizer, key_weight, value_weight, out_cotangent, lengths):
        tokens, width = layer_input.shape[1:]
        heads = gates.shape[2]
        groups = heads // PAIR
        rows = width // (2 * nx * nctx)
        srows = DK // nctx
        wide = PAIR * 2 * DK
        state = lambda: pltpu.VMEM((groups, nctx, PAIR, srows, 2 * DK), F32)
        dma = lambda *shape: pltpu.SemaphoreType.DMA(shape)
        scratch = [
            pltpu.VMEM((tokens, width), BF16),
            pltpu.VMEM((heads, width, 2 * DK), BF16),
            pltpu.VMEM((heads, tokens, DK), BF16),
            pltpu.VMEM((heads, tokens, DK), BF16),
            pltpu.VMEM((tokens, DK), F32),
            pltpu.VMEM((heads, tokens), F32),
            pltpu.VMEM((heads, tokens), F32),
            pltpu.VMEM((heads, tokens), F32),
            pltpu.VMEM((heads, tokens), F32),
            pltpu.VMEM((heads, 2 * DK), F32),
            pltpu.VMEM((nctx, heads, 2 * DK), F32),
            pltpu.VMEM((heads, 2, tokens, 2 * DK), BF16),
            pltpu.VMEM((heads, 2, DK, tokens), BF16),
            pltpu.VMEM((heads, tokens, tokens), F32),
            pltpu.VMEM((heads, tokens, tokens), F32),
            pltpu.VMEM((heads, DK, tokens), F32),
            pltpu.VMEM((heads, tokens, DK), F32),
            pltpu.VMEM((heads, tokens, 2 * DK), F32),
            state(), state(), state(), state(), state(), state(),
            pltpu.VMEM((tokens, width // 2), F32),
            pltpu.VMEM((tokens, width // 2), F32),
            pltpu.VMEM((width // 2, 2 * tokens), BF16),
            pltpu.VMEM((groups, 2 * tokens, wide), BF16),
            pltpu.VMEM((groups, tokens, wide), F32),
            pltpu.VMEM((groups, tokens, wide), F32),
            pltpu.VMEM((groups, nx, nz, ny, rows, wide), F32),
        ]
        count = {"x": nx, "z": nz, "y": ny}
        for order, rws, lns in (("xyz", rows // 2, 3 * DK), ("yzx", rows // 2, 3 * DK), ("zxy", rows, DK)):
            for n in range(3):
                left = tuple(count[a] for a in "xzy" if a not in order[: n + 1])
                scratch.append(pltpu.VMEM((groups, count[order[n]] - 1) + left + (rws, lns), F32))
        scratch += [dma(3), dma(heads), dma(2), dma(2), dma(2, groups)]
        scratch += [dma(groups)] * 8 + [dma(3, 3, groups)] * 2
        any_space = pl.BlockSpec(memory_space=pl.ANY)
        vmem = pl.BlockSpec(memory_space=pltpu.VMEM)
        smem = pl.BlockSpec(memory_space=pltpu.SMEM)
        return pl.pallas_call(
            functools.partial(mesa_kernel, (nx, nz, ny, heads, tokens, width)),
            out_shape=(
                jax.ShapeDtypeStruct((1, tokens, width), BF16),
                jax.ShapeDtypeStruct((1, tokens, heads * DK), F32),
                jax.ShapeDtypeStruct((rows, heads * DK), F32),
                jax.ShapeDtypeStruct((rows, heads * DK), F32),
            ),
            in_specs=[any_space, any_space, vmem, smem, any_space, any_space, any_space, smem],
            out_specs=(vmem, vmem, vmem, vmem),
            scratch_shapes=scratch,
            compiler_params=pltpu.CompilerParams(
                collective_id=0, has_side_effects=True, vmem_limit_bytes=63 << 20
            ),
            name="mesa_backward",
        )(layer_input, queries, gates, regularizer, key_weight, value_weight, out_cotangent, lengths)

    in_specs = (
        P("dp", "ctx", None),
        P("dp", "ctx", None),
        P("dp", "ctx", None),
        P(),
        P(),
        P(),
        P("dp", "ctx", None),
        P("dp", "ctx"),
    )
    out_specs = (
        P("dp", "ctx", None),
        P("dp", "ctx", None),
        P(("dp", "ctx"), None),
        P(("dp", "ctx"), None),
    )
    return jax.shard_map(body, mesh=mesh, in_specs=in_specs, out_specs=out_specs, check_vma=False)
```

```python
import functools

import jax
import jax.numpy as jnp
from jax import lax
from jax.experimental import pallas as pl
from jax.experimental.pallas import tpu as pltpu
from jax.sharding import PartitionSpec as P

ITERS = 4
TINY = 1e-06
DK = 128
PAIR = 2
F32 = jnp.float32
BF16 = jnp.bfloat16
MESH = pl.DeviceIdType.MESH


def split(a):
    high = a.astype(BF16)
    return high, (a - high.astype(F32)).astype(BF16)


def dot(a, b):
    return jnp.dot(a, b, preferred_element_type=F32)


def left3(parts):
    high, low = parts
    return jnp.concatenate([high, low, high], axis=1)


def right3(parts):
    high, low = parts
    return jnp.concatenate([high, high, low], axis=0)


def dot3(a, b):
    return dot(left3(a), right3(b))


def pack(sym):
    half = DK // 2
    row = lax.broadcasted_iota(jnp.int32, (half, DK), 0)
    lane = lax.broadcasted_iota(jnp.int32, (half, DK), 1)
    low = pltpu.roll(sym[half:], half, 1)
    diag = jnp.sum(jnp.where(lane == row, low, 0.0), axis=0, keepdims=True)
    return jnp.where(lane < row, low, sym[0:half]), diag


def unpack(packed, diag):
    half = DK // 2
    row = lax.broadcasted_iota(jnp.int32, (half, DK), 0)
    lane = lax.broadcasted_iota(jnp.int32, (half, DK), 1)
    diag = pltpu.roll(jnp.broadcast_to(diag, (half, DK)), half, 1)
    upper = jnp.where(lane > row, packed, 0.0)
    lower = pltpu.roll(jnp.where(lane < row, packed, 0.0), half, 1)
    off = jnp.concatenate([upper, lower], axis=0)
    on = jnp.concatenate(
        [jnp.where(lane == row, packed, 0.0), jnp.where(lane == row + half, diag, 0.0)], axis=0
    )
    return off + off.T + on


def mesa_kernel(
    sizes,
    x_ref, q_ref, gates_ref, reg_ref, wk_ref, wv_ref, g_ref, len_ref,
    ig_ref, qg_ref, kwg_ref, vwg_ref,
    x_s, w_s, q_s, g_s, run_s, tot_s, sw_s, ew_s, fac_snd, fac_rcv,
    kv_s, kt_s, dt_s, vs_s, rhs_s, ewc_s, loc_s,
    snd1, rcv1, rcv2, snd3, rcv3, rcv4, tot_snd, tot_rcv, carry_s,
    xs_snd, xs_rcv, xt_s, gr_s, sib_snd, sib_rcv, wp_s,
    ra0, ra1, ra2, ra3, rb0, rb1, rb2, rb3, rc0, rc1, rc2, rc3,
    ld_sem, w_sem, fac_sem, x_sem, sib_sem, s1, r1, s2, r2, s3, r3, s4, r4, ts, tr, rs_snd, rs_rcv,
):
    nx, nz, ny, heads, tokens, width = sizes
    nctx = nz * ny
    groups = heads // PAIR
    per = 24 // ny
    gram_rows, pair_rows = DK // 2 // ny, DK // ny
    xb = width // (2 * nx)
    rows = xb // nctx
    half = rows // 2
    dp, ctx = lax.axis_index("dp"), lax.axis_index("ctx")
    mx, mc = lax.div(dp, 2), lax.rem(dp, 2)
    mz, my = lax.div(ctx, ny), lax.rem(ctx, ny)
    sib = mx * 2 + (1 - mc)

    barrier = pltpu.get_barrier_semaphore()
    for o in range(1, nctx):
        pl.semaphore_signal(barrier, inc=1, device_id=(dp, lax.rem(ctx + o, nctx)), device_id_type=MESH)
    pl.semaphore_signal(barrier, inc=1, device_id=(sib, ctx), device_id_type=MESH)
    for o in range(1, nx):
        pl.semaphore_signal(
            barrier, inc=1, device_id=(lax.rem(mx + o, nx) * 2 + mc, ctx), device_id_type=MESH
        )

    pltpu.make_async_copy(x_ref.at[0], x_s, ld_sem.at[0]).start()
    for h in range(heads):
        cols = pl.ds(h * DK, DK)
        pltpu.make_async_copy(wk_ref.at[:, cols], w_s.at[h, :, pl.ds(0, DK)], w_sem.at[h]).start()
        pltpu.make_async_copy(wv_ref.at[:, cols], w_s.at[h, :, pl.ds(DK, DK)], w_sem.at[h]).start()
    for h in range(heads):
        cols = pl.ds(h * DK, DK)
        pltpu.make_async_copy(g_ref.at[0, :, cols], g_s.at[h], ld_sem.at[1]).start()
        pltpu.make_async_copy(q_ref.at[0, :, cols], q_s.at[h], ld_sem.at[2]).start()

    length = len_ref[0, 0]
    run = jnp.log(gates_ref[0])
    lane = lax.broadcasted_iota(jnp.int32, (heads, tokens), 1)
    step = 1
    while step < tokens:
        run = run + jnp.where(lane >= step, pltpu.roll(run, step, 1), 0.0)
        step *= 2
    total = jnp.broadcast_to(run[:, tokens - 1 : tokens], (heads, tokens))
    run_s[...] = run
    tot_s[...] = total
    sw_s[...] = jnp.exp(run)
    ew_s[...] = jnp.exp(total - run)
    fac_snd[...] = jnp.exp(total[:, 0:DK])

    mask_rows = (lax.broadcasted_iota(jnp.int32, (tokens, 2 * DK), 0) < length).astype(F32)
    mask_lane = (lax.broadcasted_iota(jnp.int32, (1, tokens), 1) < length).astype(F32)

    def across_y(src, dst, g, send, recv):
        for o in range(1, ny):
            to = lax.rem(my + o, ny)
            pltpu.make_async_remote_copy(
                src_ref=src.at[g, to], dst_ref=dst.at[g, my], send_sem=send.at[g], recv_sem=recv.at[g],
                device_id=(dp, mz * ny + to), device_id_type=MESH,
            ).start()
        pltpu.make_async_copy(src.at[g, my], dst.at[g, my], recv.at[g]).start()

    def wait_all(buf, sem):
        pltpu.make_async_copy(buf, buf, sem).wait()

    def wait_sent(buf, g, sem):
        part = buf.at[g, pl.ds(0, ny - 1)]
        pltpu.make_async_copy(part, part, sem.at[g]).wait()

    def store_state(buf, g, grams, pairs):
        head = lax.broadcasted_iota(jnp.int32, (heads, DK), 0)
        diags = jnp.zeros((heads, DK), F32)
        for i in range(PAIR):
            packed, diag = pack(grams[i])
            diags = jnp.where(head == g * PAIR + i, diag, diags)
            for to in range(ny):
                buf[g, to, i * per : i * per + per // 3] = packed[
                    to * gram_rows : (to + 1) * gram_rows
                ].reshape(per // 3, 8, DK)
                buf[g, to, i * per + per // 3 : (i + 1) * per] = pairs[i][
                    to * pair_rows : (to + 1) * pair_rows
                ].reshape(2 * per // 3, 8, DK)
        for to in range(ny):
            buf[g, to, PAIR * per] = diags

    def load_state(buf, g, i):
        head = lax.broadcasted_iota(jnp.int32, (heads, DK), 0)
        diag = jnp.sum(jnp.where(head == g * PAIR + i, buf[g, 0, PAIR * per], 0.0), axis=0, keepdims=True)
        packed = jnp.concatenate(
            [buf[g, at, i * per : i * per + per // 3].reshape(gram_rows, DK) for at in range(ny)], axis=0
        )
        pair = jnp.concatenate(
            [buf[g, at, i * per + per // 3 : (i + 1) * per].reshape(pair_rows, DK) for at in range(ny)],
            axis=0,
        )
        return unpack(packed, diag), pair

    def factors(c, g):
        return [fac_rcv[c, pl.ds(g * PAIR + i, 1), :] for i in range(PAIR)] + [fac_rcv[c]]

    def decayed(factor, tiles):
        scaled = [tiles[i * per : (i + 1) * per] * factor[i] for i in range(PAIR)]
        return jnp.concatenate(scaled + [tiles[PAIR * per :] * factor[PAIR]], axis=0)

    def project(g):
        grams, pairs = [], []
        for i in range(PAIR):
            h = g * PAIR + i
            wait_all(w_s.at[h], w_sem.at[h])
            kv = dot(x_s[...], w_s[h]) * mask_rows
            parts = split(kv)
            kv_s[h, 0], kv_s[h, 1] = parts
            kt = kv[:, 0:DK].T
            kt_s[h, 0], kt_s[h, 1] = split(kt)
            state = dot3(split(kt * ew_s[pl.ds(h, 1), :]), parts)
            grams.append(state[:, 0:DK])
            pairs.append(state[:, DK:])
        store_state(snd1, g, grams, pairs)

    def tables(g):
        for i in range(PAIR):
            h = g * PAIR + i
            run_row = run_s[pl.ds(h, 1), :]
            run_col = jnp.broadcast_to(run_row, (DK, tokens)).T
            ewc_s[h] = jnp.exp(tot_s[pl.ds(h, 1), :][:, 0:DK] - run_col)
            gap = run_row - jnp.concatenate([run_col] * (tokens // DK), axis=1)
            later = lax.broadcasted_iota(jnp.int32, (tokens, tokens), 1) >= lax.broadcasted_iota(
                jnp.int32, (tokens, tokens), 0
            )
            table = jnp.exp(jnp.where(later, gap, -1e30))
            dt_s[h] = table
            gt = ((g_s[h].astype(F32)).T * mask_lane).astype(BF16)
            v_both = jnp.concatenate([kv_s[h, 0, :, DK:], kv_s[h, 1, :, DK:]], axis=1)
            scores = dot(v_both, jnp.concatenate([gt, gt], axis=0)) * table
            vs_s[h] = scores
            rhs_s[h] = dot3((kt_s[h, 0], kt_s[h, 1]), split(scores))

    def prefix_y(buf, g, back):
        held = None
        for at in reversed(range(ny)) if back else range(ny):
            mine = buf[g, at]
            if held is None:
                buf[g, at] = jnp.zeros_like(mine)
                held = mine
            else:
                buf[g, at] = held
                held = decayed(factors(mz * ny + at, g), held) + mine
        tot_snd[back, g] = held
        for o in range(1, nz):
            to = lax.rem(mz + o, nz)

            @pl.when(to < mz if back else to > mz)
            def _():
                total_copy(back, g, to).start()

    def total_copy(back, g, to):
        return pltpu.make_async_remote_copy(
            src_ref=tot_snd.at[back, g], dst_ref=tot_rcv.at[back, g, mz],
            send_sem=ts.at[back, g, to], recv_sem=tr.at[back, g, mz],
            device_id=(dp, to * ny + my), device_id_type=MESH,
        )

    def prefix_z(buf, g, back):
        carry_s[...] = jnp.zeros_like(carry_s)
        for at in reversed(range(nz)) if back else range(nz):

            @pl.when(at > mz if back else at < mz)
            def _():
                wait_all(tot_rcv.at[back, g, at], tr.at[back, g, at])
                factor = factors(at * ny, g)
                for y in range(1, ny):
                    factor = [a * b for a, b in zip(factor, factors(at * ny + y, g))]
                carry_s[...] = decayed(factor, carry_s[...]) + tot_rcv[back, g, at]

        carried = carry_s[...]
        for at in reversed(range(ny)) if back else range(ny):
            buf[g, at] = buf[g, at] + carried
            carried = decayed(factors(mz * ny + at, g), carried)

    def solve(g, between):
        state = [load_state(rcv2, g, i) for i in range(PAIR)]
        x, r, p, rr, keys, kts, big, gts = ([None] * PAIR for _ in range(8))
        for i in range(PAIR):
            h = g * PAIR + i
            qt = q_s[h].astype(F32).T
            gts[i] = ((g_s[h].astype(F32)).T * mask_lane).astype(BF16)
            gram, pair = split(state[i][0]), split(state[i][1])
            right = rhs_s[h] + sw_s[pl.ds(h, 1), :] * dot(
                jnp.concatenate(pair, axis=1), jnp.concatenate([gts[i], gts[i]], axis=0)
            )
            p[i] = r[i] = jnp.concatenate([qt, right], axis=1)
            rr[i] = jnp.sum(r[i] * r[i], axis=0, keepdims=True)
            keys[i] = (kv_s[h, 0, :, 0:DK], kv_s[h, 1, :, 0:DK])
            kts[i] = (kt_s[h, 0], kt_s[h, 1])
            big[i] = tuple(jnp.concatenate([a, b], axis=0) for a, b in zip(keys[i], gram))
        for it in range(ITERS):
            last = it == ITERS - 1
            for i in range(PAIR):
                h = g * PAIR + i
                table = jnp.concatenate([dt_s[h]] * 2, axis=1)
                sw = jnp.concatenate([sw_s[pl.ds(h, 1), :]] * 2, axis=1)
                if last:
                    both = dot(big[i][0], p[i].astype(BF16))
                    inner = dot(kts[i][0], (both[0:tokens] * table).astype(BF16))
                else:
                    both = dot3(big[i], split(p[i]))
                    inner = dot3(kts[i], split(both[0:tokens] * table))
                image = reg_ref[h] * p[i] + sw * both[tokens:] + inner
                size = rr[i] / (jnp.sum(p[i] * image, axis=0, keepdims=True) + TINY)
                x[i] = size * p[i] if it == 0 else x[i] + size * p[i]
                if not last:
                    r[i] = r[i] - size * image
                    following = jnp.sum(r[i] * r[i], axis=0, keepdims=True)
                    p[i] = r[i] + (following / (rr[i] + TINY)) * p[i]
                    rr[i] = following
            between[it]()
        grams, pairs = [], []
        for i in range(PAIR):
            h = g * PAIR + i
            xt, yt = x[i][:, 0:tokens], x[i][:, tokens:]
            xn, yn = xt.T, yt.T
            qg_ref[0, :, pl.ds(pl.multiple_of(h * DK, DK), DK)] = yn
            gn = (g_s[h].astype(F32) * mask_rows[:, 0:DK]).astype(BF16)
            y_high, y_low = split(yn)
            yg = (
                jnp.concatenate([y_high, gn], axis=1),
                jnp.concatenate([y_low, jnp.zeros_like(gn)], axis=1),
            )
            back = dot3(split(xt * sw_s[pl.ds(h, 1), :]), yg)
            grams.append(-(back[:, 0:DK] + back[:, 0:DK].T))
            pairs.append(back[:, DK:])
            table = jnp.concatenate([dt_s[h]] * 2, axis=1)
            scores = dot3(keys[i], split(x[i])) * table
            sol, adj = scores[:, 0:tokens], scores[:, tokens:]
            from_x = dot3(split(vs_s[h] - adj), split(xn))
            from_yg = dot3(split(sol), yg)
            loc_s[h] = jnp.concatenate([from_x - from_yg[:, 0:DK], from_yg[:, DK:]], axis=1)
        store_state(snd3, g, grams, pairs)

    def gradients(g):
        for i in range(PAIR):
            h = g * PAIR + i
            sym, pair_t = load_state(rcv4, g, i)
            pair = pair_t.T
            both = jnp.concatenate(
                [
                    jnp.concatenate([sym, pair_t], axis=1),
                    jnp.concatenate([pair, jnp.zeros_like(pair)], axis=1),
                ],
                axis=0,
            )
            carried = dot3((kv_s[h, 0], kv_s[h, 1]), split(both))
            decay = jnp.concatenate([ewc_s[h]] * 2, axis=1)
            grad = ((loc_s[h] + decay * carried) * mask_rows).astype(BF16)
            gr_s[g, 0:tokens, pl.ds(i * 2 * DK, 2 * DK)] = grad
            sib_snd[g, :, pl.ds(i * 2 * DK, 2 * DK)] = grad.astype(F32)

    def sib_copy(g):
        return pltpu.make_async_remote_copy(
            src_ref=sib_snd.at[g], dst_ref=sib_rcv.at[g], send_sem=sib_sem.at[0, g], recv_sem=sib_sem.at[1, g],
            device_id=(sib, ctx), device_id_type=MESH,
        )

    me = {"x": mx, "z": mz, "y": my}
    count = {"x": nx, "z": nz, "y": ny}
    parts = [
        (order, rws, lns, bufs)
        for (order, rws, lns), bufs in zip(
            scatter_parts(rows), ((ra0, ra1, ra2, ra3), (rb0, rb1, rb2, rb3), (rc0, rc1, rc2, rc3))
        )
    ]

    def device(axis, at):
        place = dict(me)
        place[axis] = at
        return (place["x"] * 2 + mc, place["z"] * ny + place["y"])

    def chunk(n, part, g, at, side=None):
        order, rws, lns, bufs = parts[part]
        left = [a for a in "xzy" if a not in order[:n]]
        spot = tuple(at if a == order[n] else slice(None) for a in left)
        if side is not None:
            cut = halved(order, count)
            spot = tuple(
                pl.ds(side * (count[a] // 2), count[a] // 2) if a == cut else b for a, b in zip(left, spot)
            )
        if n == 0:
            return wp_s.at[(g,) + spot + (rws, lns)]
        return bufs[n].at[(g, 0) + spot]

    def send(src, dst, part, n, g, axis, to):
        pltpu.make_async_remote_copy(
            src_ref=src, dst_ref=dst, send_sem=rs_snd.at[part, n, g], recv_sem=rs_rcv.at[part, n, g],
            device_id=device(axis, to), device_id_type=MESH,
        ).start()

    def sides(axis):
        return lax.rem(me[axis] + 1, count[axis]), lax.rem(me[axis] + count[axis] - 1, count[axis])

    def scatter_far(g):
        for part, (order, rws, lns, bufs) in enumerate(parts):
            axis = order[0]
            if count[axis] == 4:
                for side, to in enumerate(sides(axis)):
                    far = lax.rem(me[axis] + 2, 4)
                    send(chunk(0, part, g, far, side), bufs[0].at[g, side], part, 0, g, axis, to)

    def scatter_near(g):
        for part, (order, rws, lns, bufs) in enumerate(parts):
            axis = order[0]
            if count[axis] == 4:
                wait_all(bufs[0].at[g], rs_rcv.at[part, 0, g])
                for side, to in enumerate(sides(axis)):
                    half_ref = chunk(0, part, g, to, side)
                    half_ref[...] = half_ref[...] + bufs[0][g, side]
                    send(chunk(0, part, g, to), bufs[1].at[g, side], part, 1, g, axis, to)
            else:
                scatter_direct(0, part, g)

    def scatter_direct(n, part, g):
        order, rws, lns, bufs = parts[part]
        axis = order[n]
        for o in range(1, count[axis]):
            to = lax.rem(me[axis] + o, count[axis])
            send(chunk(n, part, g, to), bufs[n + 1].at[g, o - 1], part, n + 1, g, axis, to)

    def scatter_start(n, g):
        for part in range(3):
            scatter_direct(n, part, g)

    def scatter_add(n, g):
        for part, (order, rws, lns, bufs) in enumerate(parts):
            summed = chunk(n, part, g, me[order[n]])[...]
            if count[order[n]] > 1:
                wait_all(bufs[n + 1].at[g], rs_rcv.at[part, n + 1, g])
                for o in range(bufs[n + 1].shape[1]):
                    summed = summed + bufs[n + 1][g, o]
            if n < 2:
                bufs[n + 1][g, 0] = summed
            else:
                first = pl.ds(pl.multiple_of(g * PAIR * DK, DK), DK)
                second = pl.ds(pl.multiple_of(g * PAIR * DK + DK, DK), DK)
                if part < 2:
                    kwg_ref[rws, first] = summed[:, 0:DK]
                    vwg_ref[rws, first] = summed[:, DK : 2 * DK]
                    kwg_ref[rws, second] = summed[:, 2 * DK :]
                else:
                    vwg_ref[rws, second] = summed

    def weight_part(g):
        sib_copy(g).wait_recv()
        gr_s[g, tokens:, :] = sib_rcv[g].astype(BF16)
        for k in range(nx):
            out = dot(xt_s[k * xb : (k + 1) * xb, :], gr_s[g])
            wp_s[g, k] = out.reshape(nz, ny, rows, PAIR * 2 * DK)
        scatter_far(g)

    def input_gradient():
        def columns(n, carry):
            span = pl.ds(pl.multiple_of(n * 256, 256), 256)
            total = None
            for h in range(heads):
                grad = gr_s[h // PAIR, 0:tokens, (h % PAIR) * 2 * DK : (h % PAIR + 1) * 2 * DK]
                term = lax.dot_general(
                    grad, w_s[h, span, :], (((1,), (1,)), ((), ())), preferred_element_type=F32
                )
                total = term if total is None else total + term
            ig_ref[0, :, span] = total.astype(BF16)
            return carry

        lax.fori_loop(0, width // 256, columns, 0)

    wait_all(x_s, ld_sem.at[0])
    project(0)
    pl.semaphore_wait(barrier, nctx - 1 + 1 + nx - 1)
    for o in range(1, nctx):
        to = lax.rem(ctx + o, nctx)
        pltpu.make_async_remote_copy(
            src_ref=fac_snd, dst_ref=fac_rcv.at[ctx], send_sem=fac_sem.at[0], recv_sem=fac_sem.at[1],
            device_id=(dp, to), device_id_type=MESH,
        ).start()
    pltpu.make_async_copy(fac_snd, fac_rcv.at[ctx], fac_sem.at[1]).start()
    across_y(snd1, rcv1, 0, s1, r1)

    def project_next(g, carry):
        project(g)
        across_y(snd1, rcv1, g, s1, r1)
        return carry

    lax.fori_loop(1, groups, project_next, 0)

    for k in range(nx):
        theirs = pl.ds(pl.multiple_of(k * 2 * xb + (1 - mc) * xb, xb), xb)
        xs_snd[:, k * xb : (k + 1) * xb] = x_s[:, theirs].astype(F32)
    x_copy = pltpu.make_async_remote_copy(
        src_ref=xs_snd, dst_ref=xs_rcv, send_sem=x_sem.at[0], recv_sem=x_sem.at[1],
        device_id=(sib, ctx), device_id_type=MESH,
    )
    x_copy.start()
    wait_all(g_s, ld_sem.at[1])
    wait_all(q_s, ld_sem.at[2])

    wait_all(fac_rcv, fac_sem.at[1])

    def during(s, first, fn):
        @pl.when(jnp.logical_and(s >= first, s < first + groups))
        def _():
            fn(s - first)

    def forward_y(g):
        wait_all(rcv1.at[g], r1.at[g])
        prefix_y(rcv1, g, 0)

    def forward_z(g):
        prefix_z(rcv1, g, 0)
        across_y(rcv1, rcv2, g, s2, r2)

    def backward_y(g):
        wait_all(rcv3.at[g], r3.at[g])
        prefix_y(rcv3, g, 1)

    def backward_z(g):
        prefix_z(rcv3, g, 1)
        across_y(rcv3, rcv4, g, s4, r4)

    def tables_next(s, carry):
        during(s, 0, tables)
        during(s, 0, forward_y)
        during(s, 1, forward_z)
        return carry

    lax.fori_loop(0, groups + 1, tables_next, 0)
    for k in range(nx):
        mine = pl.ds(pl.multiple_of(k * 2 * xb + mc * xb, xb), xb)
        xt_s[k * xb : (k + 1) * xb, 0:tokens] = x_s[:, mine].astype(F32).T.astype(BF16)
    x_copy.wait_recv()
    for k in range(nx):
        xt_s[k * xb : (k + 1) * xb, tokens:] = xs_rcv[:, k * xb : (k + 1) * xb].T.astype(BF16)

    def backward_grads(g):
        wait_all(rcv4.at[g], r4.at[g])
        gradients(g)
        sib_copy(g).start()

    def reduce_two(g):
        scatter_add(0, g)
        scatter_start(1, g)

    def reduce_three(g):
        scatter_add(1, g)
        scatter_start(2, g)

    def reduce_last(g):
        scatter_add(2, g)

    def steps(s):
        def zero():
            during(s, 3, weight_part)

        def one():
            during(s, 2, backward_z)
            during(s, 5, reduce_three)

        def two():
            during(s, 4, reduce_two)

        def three():
            during(s, 1, backward_y)
            during(s, 3, scatter_near)

        def end():
            during(s, 2, backward_grads)
            during(s, 6, reduce_last)

        return (zero, one, two, three), end

    def with_solve(s, carry):
        between, end = steps(s)
        wait_all(rcv2.at[s], r2.at[s])
        solve(s, between)
        across_y(snd3, rcv3, s, s3, r3)
        end()
        return carry

    def without_solve(s, carry):
        between, end = steps(s)
        for fn in between:
            fn()
        pl.when(s == groups + 2)(input_gradient)
        end()
        return carry

    lax.fori_loop(0, groups, with_solve, 0)
    lax.fori_loop(groups, groups + 6, without_solve, 0)

    sent = pltpu.make_async_copy(
        fac_rcv.at[pl.ds(0, nctx - 1)], fac_rcv.at[pl.ds(0, nctx - 1)], fac_sem.at[0]
    )
    sent.wait()
    x_copy.wait_send()

    def drain(g, carry):
        wait_sent(snd1, g, s1)
        wait_sent(rcv1, g, s2)
        wait_sent(snd3, g, s3)
        wait_sent(rcv3, g, s4)
        sib_copy(g).wait_send()
        for part, (order, rws, lns, bufs) in enumerate(parts):
            for n in range(4):
                if count[order[max(n - 1, 0)]] > 1 and (n > 0 or count[order[0]] == 4):
                    wait_all(bufs[n].at[g], rs_snd.at[part, n, g])
        for back in range(2):
            for o in range(1, nz):
                to = lax.rem(mz + o, nz)

                @pl.when(to < mz if back else to > mz)
                def _():
                    total_copy(back, g, to).wait_send()

        return carry

    lax.fori_loop(0, groups, drain, 0)


def scatter_parts(rows):
    return (
        ("xzy", pl.ds(0, rows // 2), pl.ds(0, 3 * DK)),
        ("zxy", pl.ds(rows // 2, rows // 2), pl.ds(0, 3 * DK)),
        ("yxz", pl.ds(0, rows), pl.ds(3 * DK, DK)),
    )


def halved(order, count):
    return [a for a in "xzy" if a != order[0] and count[a] % 2 == 0][0]


def solution(mesh):
    nx = mesh.shape["dp"] // 2
    nctx = mesh.shape["ctx"]
    ny = min(nctx, 4)
    nz = nctx // ny

    def body(layer_input, queries, gates, regularizer, key_weight, value_weight, out_cotangent, lengths):
        tokens, width = layer_input.shape[1:]
        heads = gates.shape[2]
        groups = heads // PAIR
        rows = width // (2 * nx * nctx)
        tiles = PAIR * 24 // ny + 1
        wide = PAIR * 2 * DK
        state = lambda: pltpu.VMEM((groups, ny, tiles, 8, DK), F32)
        dma = lambda *shape: pltpu.SemaphoreType.DMA(shape)
        scratch = [
            pltpu.VMEM((tokens, width), BF16),
            pltpu.VMEM((heads, width, 2 * DK), BF16),
            pltpu.VMEM((heads, tokens, DK), BF16),
            pltpu.VMEM((heads, tokens, DK), BF16),
            pltpu.VMEM((heads, tokens), F32),
            pltpu.VMEM((heads, tokens), F32),
            pltpu.VMEM((heads, tokens), F32),
            pltpu.VMEM((heads, tokens), F32),
            pltpu.VMEM((heads, DK), F32),
            pltpu.VMEM((nctx, heads, DK), F32),
            pltpu.VMEM((heads, 2, tokens, 2 * DK), BF16),
            pltpu.VMEM((heads, 2, DK, tokens), BF16),
            pltpu.VMEM((heads, tokens, tokens), F32),
            pltpu.VMEM((heads, tokens, tokens), F32),
            pltpu.VMEM((heads, DK, tokens), F32),
            pltpu.VMEM((heads, tokens, DK), F32),
            pltpu.VMEM((heads, tokens, 2 * DK), F32),
            state(), state(), state(), state(), state(), state(),
            pltpu.VMEM((2, groups, tiles, 8, DK), F32),
            pltpu.VMEM((2, groups, nz, tiles, 8, DK), F32),
            pltpu.VMEM((tiles, 8, DK), F32),
            pltpu.VMEM((tokens, width // 2), F32),
            pltpu.VMEM((tokens, width // 2), F32),
            pltpu.VMEM((width // 2, 2 * tokens), BF16),
            pltpu.VMEM((groups, 2 * tokens, wide), BF16),
            pltpu.VMEM((groups, tokens, wide), F32),
            pltpu.VMEM((groups, tokens, wide), F32),
            pltpu.VMEM((groups, nx, nz, ny, rows, wide), F32),
        ]
        count = {"x": nx, "z": nz, "y": ny}
        for order, rws, lns in scatter_parts(rows):
            cut = halved(order, count)
            shape = tuple(count[a] // 2 if a == cut else count[a] for a in "xzy" if a != order[0])
            scratch.append(pltpu.VMEM((groups, 2) + shape + (rws.size, lns.size), F32))
            for n in range(3):
                slots = 2 if n == 0 and count[order[0]] == 4 else max(count[order[n]] - 1, 1)
                left = tuple(count[a] for a in "xzy" if a not in order[: n + 1])
                scratch.append(pltpu.VMEM((groups, slots) + left + (rws.size, lns.size), F32))
        scratch += [dma(3), dma(heads), dma(2), dma(2), dma(2, groups)]
        scratch += [dma(groups)] * 8 + [dma(2, groups, nz)] * 2 + [dma(3, 4, groups)] * 2
        any_space = pl.BlockSpec(memory_space=pl.ANY)
        vmem = pl.BlockSpec(memory_space=pltpu.VMEM)
        smem = pl.BlockSpec(memory_space=pltpu.SMEM)
        return pl.pallas_call(
            functools.partial(mesa_kernel, (nx, nz, ny, heads, tokens, width)),
            out_shape=(
                jax.ShapeDtypeStruct((1, tokens, width), BF16),
                jax.ShapeDtypeStruct((1, tokens, heads * DK), F32),
                jax.ShapeDtypeStruct((rows, heads * DK), F32),
                jax.ShapeDtypeStruct((rows, heads * DK), F32),
            ),
            in_specs=[any_space, any_space, vmem, smem, any_space, any_space, any_space, smem],
            out_specs=(vmem, vmem, vmem, vmem),
            scratch_shapes=scratch,
            compiler_params=pltpu.CompilerParams(
                collective_id=0, has_side_effects=True, vmem_limit_bytes=63 << 20
            ),
            name="mesa_backward",
        )(layer_input, queries, jnp.swapaxes(gates, 1, 2), regularizer, key_weight, value_weight, out_cotangent, lengths)

    in_specs = (
        P("dp", "ctx", None),
        P("dp", "ctx", None),
        P("dp", "ctx", None),
        P(),
        P(),
        P(),
        P("dp", "ctx", None),
        P("dp", "ctx"),
    )
    out_specs = (
        P("dp", "ctx", None),
        P("dp", "ctx", None),
        P(("dp", "ctx"), None),
        P(("dp", "ctx"), None),
    )
    return jax.shard_map(body, mesh=mesh, in_specs=in_specs, out_specs=out_specs, check_vma=False)
```

```python
import functools

import jax
import jax.numpy as jnp
from jax import lax
from jax.experimental import pallas as pl
from jax.experimental.pallas import tpu as pltpu
from jax.sharding import PartitionSpec as P

ITERS = 4
TINY = 1e-06
DK = 128
PAIR = 2
F32 = jnp.float32
BF16 = jnp.bfloat16
MESH = pl.DeviceIdType.MESH


def split(a):
    high = a.astype(BF16)
    return high, (a - high.astype(F32)).astype(BF16)


def dot(a, b):
    return jnp.dot(a, b, preferred_element_type=F32)


def left3(parts):
    high, low = parts
    return jnp.concatenate([high, low, high], axis=1)


def right3(parts):
    high, low = parts
    return jnp.concatenate([high, high, low], axis=0)


def dot3(a, b):
    return dot(left3(a), right3(b))


def pack(sym):
    half = DK // 2
    row = lax.broadcasted_iota(jnp.int32, (half, DK), 0)
    lane = lax.broadcasted_iota(jnp.int32, (half, DK), 1)
    low = pltpu.roll(sym[half:], half, 1)
    diag = jnp.sum(jnp.where(lane == row, low, 0.0), axis=0, keepdims=True)
    return jnp.where(lane < row, low, sym[0:half]), diag


def unpack(packed, diag):
    half = DK // 2
    row = lax.broadcasted_iota(jnp.int32, (half, DK), 0)
    lane = lax.broadcasted_iota(jnp.int32, (half, DK), 1)
    diag = pltpu.roll(jnp.broadcast_to(diag, (half, DK)), half, 1)
    upper = jnp.where(lane > row, packed, 0.0)
    lower = pltpu.roll(jnp.where(lane < row, packed, 0.0), half, 1)
    off = jnp.concatenate([upper, lower], axis=0)
    on = jnp.concatenate(
        [jnp.where(lane == row, packed, 0.0), jnp.where(lane == row + half, diag, 0.0)], axis=0
    )
    return off + off.T + on


def mesa_kernel(
    sizes,
    x_ref, q_ref, gates_ref, reg_ref, wk_ref, wv_ref, g_ref, len_ref,
    ig_ref, qg_ref, kwg_ref, vwg_ref,
    x_s, w_s, q_s, g_s, run_s, tot_s, sw_s, ew_s, fac_snd, fac_rcv,
    kv_s, kt_s, dt_s, vs_s, rhs_s, ewc_s, loc_s,
    snd1, rcv1, rcv2, snd3, rcv3, rcv4, tot_snd, tot_rcv, carry_s,
    xs_snd, xs_rcv, xt_s, gr_s, sib_snd, sib_rcv, wp_s,
    ra0, ra1, ra2, ra3, rb0, rb1, rb2, rb3, rc0, rc1, rc2, rc3,
    ld_sem, w_sem, fac_sem, x_sem, sib_sem, s1, r1, s2, r2, s3, r3, s4, r4, ts, tr, rs_snd, rs_rcv,
):
    nx, nz, ny, heads, tokens, width = sizes
    nctx = nz * ny
    groups = heads // PAIR
    per = 24 // ny
    gram_rows, pair_rows = DK // 2 // ny, DK // ny
    xb = width // (2 * nx)
    rows = xb // nctx
    half = rows // 2
    dp, ctx = lax.axis_index("dp"), lax.axis_index("ctx")
    mx, mc = lax.div(dp, 2), lax.rem(dp, 2)
    mz, my = lax.div(ctx, ny), lax.rem(ctx, ny)
    sib = mx * 2 + (1 - mc)

    barrier = pltpu.get_barrier_semaphore()
    for o in range(1, nctx):
        pl.semaphore_signal(barrier, inc=1, device_id=(dp, lax.rem(ctx + o, nctx)), device_id_type=MESH)
    pl.semaphore_signal(barrier, inc=1, device_id=(sib, ctx), device_id_type=MESH)
    for o in range(1, nx):
        pl.semaphore_signal(
            barrier, inc=1, device_id=(lax.rem(mx + o, nx) * 2 + mc, ctx), device_id_type=MESH
        )

    pltpu.make_async_copy(x_ref.at[0], x_s, ld_sem.at[0]).start()
    for h in range(heads):
        cols = pl.ds(h * DK, DK)
        pltpu.make_async_copy(wk_ref.at[:, cols], w_s.at[h, :, pl.ds(0, DK)], w_sem.at[h]).start()
        pltpu.make_async_copy(wv_ref.at[:, cols], w_s.at[h, :, pl.ds(DK, DK)], w_sem.at[h]).start()
    for h in range(heads):
        cols = pl.ds(h * DK, DK)
        pltpu.make_async_copy(g_ref.at[0, :, cols], g_s.at[h], ld_sem.at[1]).start()
        pltpu.make_async_copy(q_ref.at[0, :, cols], q_s.at[h], ld_sem.at[2]).start()

    length = len_ref[0, 0]
    run = jnp.log(gates_ref[0])
    lane = lax.broadcasted_iota(jnp.int32, (heads, tokens), 1)
    step = 1
    while step < tokens:
        run = run + jnp.where(lane >= step, pltpu.roll(run, step, 1), 0.0)
        step *= 2
    total = jnp.broadcast_to(run[:, tokens - 1 : tokens], (heads, tokens))
    run_s[...] = run
    tot_s[...] = total
    sw_s[...] = jnp.exp(run)
    ew_s[...] = jnp.exp(total - run)
    fac_snd[...] = jnp.exp(total[:, 0:DK])

    mask_rows = (lax.broadcasted_iota(jnp.int32, (tokens, 2 * DK), 0) < length).astype(F32)
    mask_lane = (lax.broadcasted_iota(jnp.int32, (1, tokens), 1) < length).astype(F32)

    def across_y(src, dst, g, send, recv):
        for o in range(1, ny):
            to = lax.rem(my + o, ny)
            pltpu.make_async_remote_copy(
                src_ref=src.at[g, to], dst_ref=dst.at[g, my], send_sem=send.at[g], recv_sem=recv.at[g],
                device_id=(dp, mz * ny + to), device_id_type=MESH,
            ).start()
        pltpu.make_async_copy(src.at[g, my], dst.at[g, my], recv.at[g]).start()

    def wait_all(buf, sem):
        pltpu.make_async_copy(buf, buf, sem).wait()

    def wait_sent(buf, g, sem):
        part = buf.at[g, pl.ds(0, ny - 1)]
        pltpu.make_async_copy(part, part, sem.at[g]).wait()

    def store_state(buf, g, grams, pairs):
        head = lax.broadcasted_iota(jnp.int32, (heads, DK), 0)
        diags = jnp.zeros((heads, DK), F32)
        for i in range(PAIR):
            packed, diag = pack(grams[i])
            diags = jnp.where(head == g * PAIR + i, diag, diags)
            for to in range(ny):
                buf[g, to, i * per : i * per + per // 3] = packed[
                    to * gram_rows : (to + 1) * gram_rows
                ].reshape(per // 3, 8, DK)
                buf[g, to, i * per + per // 3 : (i + 1) * per] = pairs[i][
                    to * pair_rows : (to + 1) * pair_rows
                ].reshape(2 * per // 3, 8, DK)
        for to in range(ny):
            buf[g, to, PAIR * per] = diags

    def load_state(buf, g, i):
        head = lax.broadcasted_iota(jnp.int32, (heads, DK), 0)
        diag = jnp.sum(jnp.where(head == g * PAIR + i, buf[g, 0, PAIR * per], 0.0), axis=0, keepdims=True)
        packed = jnp.concatenate(
            [buf[g, at, i * per : i * per + per // 3].reshape(gram_rows, DK) for at in range(ny)], axis=0
        )
        pair = jnp.concatenate(
            [buf[g, at, i * per + per // 3 : (i + 1) * per].reshape(pair_rows, DK) for at in range(ny)],
            axis=0,
        )
        return unpack(packed, diag), pair

    def factors(c, g):
        return [fac_rcv[c, pl.ds(g * PAIR + i, 1), :] for i in range(PAIR)] + [fac_rcv[c]]

    def decayed(factor, tiles):
        scaled = [tiles[i * per : (i + 1) * per] * factor[i] for i in range(PAIR)]
        return jnp.concatenate(scaled + [tiles[PAIR * per :] * factor[PAIR]], axis=0)

    def project(g):
        grams, pairs = [], []
        for i in range(PAIR):
            h = g * PAIR + i
            wait_all(w_s.at[h], w_sem.at[h])
            kv = dot(x_s[...], w_s[h]) * mask_rows
            parts = split(kv)
            kv_s[h, 0], kv_s[h, 1] = parts
            kt = kv[:, 0:DK].T
            kt_s[h, 0], kt_s[h, 1] = split(kt)
            state = dot3(split(kt * ew_s[pl.ds(h, 1), :]), parts)
            grams.append(state[:, 0:DK])
            pairs.append(state[:, DK:])
        store_state(snd1, g, grams, pairs)

    def tables(g):
        for i in range(PAIR):
            h = g * PAIR + i
            run_row = run_s[pl.ds(h, 1), :]
            run_col = jnp.broadcast_to(run_row, (DK, tokens)).T
            ewc_s[h] = jnp.exp(tot_s[pl.ds(h, 1), :][:, 0:DK] - run_col)
            gap = run_row - jnp.concatenate([run_col] * (tokens // DK), axis=1)
            later = lax.broadcasted_iota(jnp.int32, (tokens, tokens), 1) >= lax.broadcasted_iota(
                jnp.int32, (tokens, tokens), 0
            )
            table = jnp.exp(jnp.where(later, gap, -1e30))
            dt_s[h] = table
            gt = ((g_s[h].astype(F32)).T * mask_lane).astype(BF16)
            v_both = jnp.concatenate([kv_s[h, 0, :, DK:], kv_s[h, 1, :, DK:]], axis=1)
            scores = dot(v_both, jnp.concatenate([gt, gt], axis=0)) * table
            vs_s[h] = scores
            rhs_s[h] = dot3((kt_s[h, 0], kt_s[h, 1]), split(scores))

    def prefix_y(buf, g, back):
        held = None
        for at in reversed(range(ny)) if back else range(ny):
            mine = buf[g, at]
            if held is None:
                buf[g, at] = jnp.zeros_like(mine)
                held = mine
            else:
                buf[g, at] = held
                held = decayed(factors(mz * ny + at, g), held) + mine
        tot_snd[back, g] = held
        for o in range(1, nz):
            to = lax.rem(mz + o, nz)

            @pl.when(to < mz if back else to > mz)
            def _():
                total_copy(back, g, to).start()

    def total_copy(back, g, to):
        return pltpu.make_async_remote_copy(
            src_ref=tot_snd.at[back, g], dst_ref=tot_rcv.at[back, g, mz],
            send_sem=ts.at[back, g, to], recv_sem=tr.at[back, g, mz],
            device_id=(dp, to * ny + my), device_id_type=MESH,
        )

    def prefix_z(buf, g, back):
        carry_s[...] = jnp.zeros_like(carry_s)
        for at in reversed(range(nz)) if back else range(nz):

            @pl.when(at > mz if back else at < mz)
            def _():
                wait_all(tot_rcv.at[back, g, at], tr.at[back, g, at])
                factor = factors(at * ny, g)
                for y in range(1, ny):
                    factor = [a * b for a, b in zip(factor, factors(at * ny + y, g))]
                carry_s[...] = decayed(factor, carry_s[...]) + tot_rcv[back, g, at]

        carried = carry_s[...]
        for at in reversed(range(ny)) if back else range(ny):
            buf[g, at] = buf[g, at] + carried
            carried = decayed(factors(mz * ny + at, g), carried)

    def solve(g, between):
        state = [load_state(rcv2, g, i) for i in range(PAIR)]
        x, r, p, rr, keys, kts, big, gts = ([None] * PAIR for _ in range(8))
        for i in range(PAIR):
            h = g * PAIR + i
            qt = q_s[h].astype(F32).T
            gts[i] = ((g_s[h].astype(F32)).T * mask_lane).astype(BF16)
            gram, pair = split(state[i][0]), split(state[i][1])
            right = rhs_s[h] + sw_s[pl.ds(h, 1), :] * dot(
                jnp.concatenate(pair, axis=1), jnp.concatenate([gts[i], gts[i]], axis=0)
            )
            p[i] = r[i] = jnp.concatenate([qt, right], axis=1)
            rr[i] = jnp.sum(r[i] * r[i], axis=0, keepdims=True)
            keys[i] = (kv_s[h, 0, :, 0:DK], kv_s[h, 1, :, 0:DK])
            kts[i] = (kt_s[h, 0], kt_s[h, 1])
            big[i] = tuple(jnp.concatenate([a, b], axis=0) for a, b in zip(keys[i], gram))
        for it in range(ITERS):
            last = it == ITERS - 1
            for i in range(PAIR):
                h = g * PAIR + i
                table = jnp.concatenate([dt_s[h]] * 2, axis=1)
                sw = jnp.concatenate([sw_s[pl.ds(h, 1), :]] * 2, axis=1)
                if last:
                    both = dot(big[i][0], p[i].astype(BF16))
                    inner = dot(kts[i][0], (both[0:tokens] * table).astype(BF16))
                else:
                    both = dot3(big[i], split(p[i]))
                    inner = dot3(kts[i], split(both[0:tokens] * table))
                image = reg_ref[h] * p[i] + sw * both[tokens:] + inner
                size = rr[i] / (jnp.sum(p[i] * image, axis=0, keepdims=True) + TINY)
                x[i] = size * p[i] if it == 0 else x[i] + size * p[i]
                if not last:
                    r[i] = r[i] - size * image
                    following = jnp.sum(r[i] * r[i], axis=0, keepdims=True)
                    p[i] = r[i] + (following / (rr[i] + TINY)) * p[i]
                    rr[i] = following
            between[it]()
        grams, pairs = [], []
        for i in range(PAIR):
            h = g * PAIR + i
            xt, yt = x[i][:, 0:tokens], x[i][:, tokens:]
            xn, yn = xt.T, yt.T
            qg_ref[0, :, pl.ds(pl.multiple_of(h * DK, DK), DK)] = yn
            gn = (g_s[h].astype(F32) * mask_rows[:, 0:DK]).astype(BF16)
            y_high, y_low = split(yn)
            yg = (
                jnp.concatenate([y_high, gn], axis=1),
                jnp.concatenate([y_low, jnp.zeros_like(gn)], axis=1),
            )
            back = dot3(split(xt * sw_s[pl.ds(h, 1), :]), yg)
            grams.append(-(back[:, 0:DK] + back[:, 0:DK].T))
            pairs.append(back[:, DK:])
            table = jnp.concatenate([dt_s[h]] * 2, axis=1)
            scores = dot3(keys[i], split(x[i])) * table
            sol, adj = scores[:, 0:tokens], scores[:, tokens:]
            from_x = dot3(split(vs_s[h] - adj), split(xn))
            from_yg = dot3(split(sol), yg)
            loc_s[h] = jnp.concatenate([from_x - from_yg[:, 0:DK], from_yg[:, DK:]], axis=1)
        store_state(snd3, g, grams, pairs)

    def gradients(g):
        for i in range(PAIR):
            h = g * PAIR + i
            sym, pair_t = load_state(rcv4, g, i)
            pair = pair_t.T
            both = jnp.concatenate(
                [
                    jnp.concatenate([sym, pair_t], axis=1),
                    jnp.concatenate([pair, jnp.zeros_like(pair)], axis=1),
                ],
                axis=0,
            )
            carried = dot3((kv_s[h, 0], kv_s[h, 1]), split(both))
            decay = jnp.concatenate([ewc_s[h]] * 2, axis=1)
            grad = ((loc_s[h] + decay * carried) * mask_rows).astype(BF16)
            gr_s[g, 0:tokens, pl.ds(i * 2 * DK, 2 * DK)] = grad
            sib_snd[g, :, pl.ds(i * 2 * DK, 2 * DK)] = grad.astype(F32)

    def sib_copy(g):
        return pltpu.make_async_remote_copy(
            src_ref=sib_snd.at[g], dst_ref=sib_rcv.at[g], send_sem=sib_sem.at[0, g], recv_sem=sib_sem.at[1, g],
            device_id=(sib, ctx), device_id_type=MESH,
        )

    me = {"x": mx, "z": mz, "y": my}
    count = {"x": nx, "z": nz, "y": ny}
    parts = [
        (order, rws, lns, bufs)
        for (order, rws, lns), bufs in zip(
            scatter_parts(rows), ((ra0, ra1, ra2, ra3), (rb0, rb1, rb2, rb3), (rc0, rc1, rc2, rc3))
        )
    ]

    def device(axis, at):
        place = dict(me)
        place[axis] = at
        return (place["x"] * 2 + mc, place["z"] * ny + place["y"])

    def chunk(n, part, g, at, side=None):
        order, rws, lns, bufs = parts[part]
        left = [a for a in "xzy" if a not in order[:n]]
        spot = tuple(at if a == order[n] else slice(None) for a in left)
        if side is not None:
            cut = halved(order, count)
            spot = tuple(
                pl.ds(side * (count[a] // 2), count[a] // 2) if a == cut else b for a, b in zip(left, spot)
            )
        if n == 0:
            return wp_s.at[(g,) + spot + (rws, lns)]
        return bufs[n].at[(g, 0) + spot]

    def send(src, dst, part, n, g, axis, to):
        pltpu.make_async_remote_copy(
            src_ref=src, dst_ref=dst, send_sem=rs_snd.at[part, n, g], recv_sem=rs_rcv.at[part, n, g],
            device_id=device(axis, to), device_id_type=MESH,
        ).start()

    def sides(axis):
        return lax.rem(me[axis] + 1, count[axis]), lax.rem(me[axis] + count[axis] - 1, count[axis])

    def scatter_far(g):
        for part, (order, rws, lns, bufs) in enumerate(parts):
            axis = order[0]
            if count[axis] == 4:
                for side, to in enumerate(sides(axis)):
                    far = lax.rem(me[axis] + 2, 4)
                    send(chunk(0, part, g, far, side), bufs[0].at[g, side], part, 0, g, axis, to)

    def scatter_near(g):
        for part, (order, rws, lns, bufs) in enumerate(parts):
            axis = order[0]
            if count[axis] == 4:
                wait_all(bufs[0].at[g], rs_rcv.at[part, 0, g])
                for side, to in enumerate(sides(axis)):
                    half_ref = chunk(0, part, g, to, side)
                    half_ref[...] = half_ref[...] + bufs[0][g, side]
                    send(chunk(0, part, g, to), bufs[1].at[g, side], part, 1, g, axis, to)
            else:
                scatter_direct(0, part, g)

    def scatter_direct(n, part, g):
        order, rws, lns, bufs = parts[part]
        axis = order[n]
        for o in range(1, count[axis]):
            to = lax.rem(me[axis] + o, count[axis])
            send(chunk(n, part, g, to), bufs[n + 1].at[g, o - 1], part, n + 1, g, axis, to)

    def scatter_start(n, g):
        for part in range(3):
            scatter_direct(n, part, g)

    def scatter_add(n, g):
        for part, (order, rws, lns, bufs) in enumerate(parts):
            summed = chunk(n, part, g, me[order[n]])[...]
            if count[order[n]] > 1:
                wait_all(bufs[n + 1].at[g], rs_rcv.at[part, n + 1, g])
                for o in range(bufs[n + 1].shape[1]):
                    summed = summed + bufs[n + 1][g, o]
            if n < 2:
                bufs[n + 1][g, 0] = summed
            else:
                first, second = (pl.ds((g * PAIR + i) * DK, DK) for i in range(PAIR))
                if part < 2:
                    kwg_ref[rws, first] = summed[:, 0:DK]
                    vwg_ref[rws, first] = summed[:, DK : 2 * DK]
                    kwg_ref[rws, second] = summed[:, 2 * DK :]
                else:
                    vwg_ref[rws, second] = summed

    def weight_part(g):
        sib_copy(g).wait_recv()
        gr_s[g, tokens:, :] = sib_rcv[g].astype(BF16)
        for k in range(nx):
            out = dot(xt_s[k * xb : (k + 1) * xb, :], gr_s[g])
            wp_s[g, k] = out.reshape(nz, ny, rows, PAIR * 2 * DK)
        scatter_far(g)

    def input_gradient():
        def columns(n, carry):
            span = pl.ds(pl.multiple_of(n * 256, 256), 256)
            total = None
            for h in range(heads):
                grad = gr_s[h // PAIR, 0:tokens, (h % PAIR) * 2 * DK : (h % PAIR + 1) * 2 * DK]
                term = lax.dot_general(
                    grad, w_s[h, span, :], (((1,), (1,)), ((), ())), preferred_element_type=F32
                )
                total = term if total is None else total + term
            ig_ref[0, :, span] = total.astype(BF16)
            return carry

        lax.fori_loop(0, width // 256, columns, 0)

    def forward_y(g):
        wait_all(rcv1.at[g], r1.at[g])
        prefix_y(rcv1, g, 0)

    def forward_z(g):
        prefix_z(rcv1, g, 0)
        across_y(rcv1, rcv2, g, s2, r2)

    def backward_y(g):
        wait_all(rcv3.at[g], r3.at[g])
        prefix_y(rcv3, g, 1)

    def backward_z(g):
        prefix_z(rcv3, g, 1)
        across_y(rcv3, rcv4, g, s4, r4)

    def backward_grads(g):
        wait_all(rcv4.at[g], r4.at[g])
        gradients(g)
        sib_copy(g).start()

    def reduce_two(g):
        scatter_add(0, g)
        scatter_start(1, g)

    def reduce_three(g):
        scatter_add(1, g)
        scatter_start(2, g)

    def reduce_last(g):
        scatter_add(2, g)

    def send_state(g):
        across_y(snd1, rcv1, g, s1, r1)

    wait_all(x_s, ld_sem.at[0])
    project(0)
    pl.semaphore_wait(barrier, nctx - 1 + 1 + nx - 1)
    for o in range(1, nctx):
        to = lax.rem(ctx + o, nctx)
        pltpu.make_async_remote_copy(
            src_ref=fac_snd, dst_ref=fac_rcv.at[ctx], send_sem=fac_sem.at[0], recv_sem=fac_sem.at[1],
            device_id=(dp, to), device_id_type=MESH,
        ).start()
    pltpu.make_async_copy(fac_snd, fac_rcv.at[ctx], fac_sem.at[1]).start()
    send_state(0)
    project(1)
    send_state(1)
    wait_all(g_s, ld_sem.at[1])
    wait_all(q_s, ld_sem.at[2])
    tables(0)
    tables(1)
    wait_all(fac_rcv, fac_sem.at[1])
    forward_y(0)
    project(2)
    forward_y(1)
    forward_z(0)
    send_state(2)
    forward_z(1)
    for k in range(nx):
        theirs = pl.ds(pl.multiple_of(k * 2 * xb + (1 - mc) * xb, xb), xb)
        xs_snd[:, k * xb : (k + 1) * xb] = x_s[:, theirs].astype(F32)
    x_copy = pltpu.make_async_remote_copy(
        src_ref=xs_snd, dst_ref=xs_rcv, send_sem=x_sem.at[0], recv_sem=x_sem.at[1],
        device_id=(sib, ctx), device_id_type=MESH,
    )
    x_copy.start()
    project(3)
    send_state(3)
    tables(2)
    tables(3)
    forward_y(2)
    for k in range(nx):
        mine = pl.ds(pl.multiple_of(k * 2 * xb + mc * xb, xb), xb)
        xt_s[k * xb : (k + 1) * xb, 0:tokens] = x_s[:, mine].astype(F32).T.astype(BF16)

    def during(s, first, fn, count=groups):
        @pl.when(jnp.logical_and(s >= first, s < first + count))
        def _():
            fn(s - first)

    def with_solve(s, carry):
        def zero():
            during(s, 3, weight_part)
            pl.when(s == 0)(lambda: forward_z(2))

        def one():
            pl.when(s == 0)(lambda: forward_y(3))
            during(s, 2, backward_z)

        def two():
            pl.when(s == 0)(lambda: forward_z(3))

        def three():
            during(s, 1, backward_y)
            during(s, 3, scatter_near)

        wait_all(rcv2.at[s], r2.at[s])
        solve(s, (zero, one, two, three))
        across_y(snd3, rcv3, s, s3, r3)
        during(s, 2, backward_grads)

        @pl.when(s == 0)
        def _():
            x_copy.wait_recv()
            for k in range(nx):
                xt_s[k * xb : (k + 1) * xb, tokens:] = xs_rcv[:, k * xb : (k + 1) * xb].T.astype(BF16)

        return carry

    lax.fori_loop(0, groups, with_solve, 0)
    backward_z(2)
    weight_part(1)
    backward_y(3)
    backward_grads(2)
    scatter_near(1)
    backward_z(3)
    weight_part(2)
    reduce_two(0)
    backward_grads(3)
    scatter_near(2)
    weight_part(3)
    reduce_two(1)
    reduce_three(0)
    input_gradient()
    scatter_near(3)
    reduce_two(2)
    reduce_three(1)
    reduce_last(0)
    reduce_two(3)
    reduce_three(2)
    reduce_last(1)
    reduce_three(3)
    reduce_last(2)
    reduce_last(3)

    sent = pltpu.make_async_copy(
        fac_rcv.at[pl.ds(0, nctx - 1)], fac_rcv.at[pl.ds(0, nctx - 1)], fac_sem.at[0]
    )
    sent.wait()
    x_copy.wait_send()

    def drain(g, carry):
        wait_sent(snd1, g, s1)
        wait_sent(rcv1, g, s2)
        wait_sent(snd3, g, s3)
        wait_sent(rcv3, g, s4)
        sib_copy(g).wait_send()
        for part, (order, rws, lns, bufs) in enumerate(parts):
            for n in range(4):
                if count[order[max(n - 1, 0)]] > 1 and (n > 0 or count[order[0]] == 4):
                    wait_all(bufs[n].at[g], rs_snd.at[part, n, g])
        for back in range(2):
            for o in range(1, nz):
                to = lax.rem(mz + o, nz)

                @pl.when(to < mz if back else to > mz)
                def _():
                    total_copy(back, g, to).wait_send()

        return carry

    lax.fori_loop(0, groups, drain, 0)


def scatter_parts(rows):
    return (
        ("xyz", pl.ds(0, rows // 2), pl.ds(0, 3 * DK)),
        ("zxy", pl.ds(rows // 2, rows // 2), pl.ds(0, 3 * DK)),
        ("yzx", pl.ds(0, rows), pl.ds(3 * DK, DK)),
    )


def halved(order, count):
    return [a for a in "xzy" if a != order[0] and count[a] % 2 == 0][0]


def solution(mesh):
    nx = mesh.shape["dp"] // 2
    nctx = mesh.shape["ctx"]
    ny = min(nctx, 4)
    nz = nctx // ny

    def body(layer_input, queries, gates, regularizer, key_weight, value_weight, out_cotangent, lengths):
        tokens, width = layer_input.shape[1:]
        heads = gates.shape[2]
        groups = heads // PAIR
        rows = width // (2 * nx * nctx)
        tiles = PAIR * 24 // ny + 1
        wide = PAIR * 2 * DK
        state = lambda: pltpu.VMEM((groups, ny, tiles, 8, DK), F32)
        dma = lambda *shape: pltpu.SemaphoreType.DMA(shape)
        scratch = [
            pltpu.VMEM((tokens, width), BF16),
            pltpu.VMEM((heads, width, 2 * DK), BF16),
            pltpu.VMEM((heads, tokens, DK), BF16),
            pltpu.VMEM((heads, tokens, DK), BF16),
            pltpu.VMEM((heads, tokens), F32),
            pltpu.VMEM((heads, tokens), F32),
            pltpu.VMEM((heads, tokens), F32),
            pltpu.VMEM((heads, tokens), F32),
            pltpu.VMEM((heads, DK), F32),
            pltpu.VMEM((nctx, heads, DK), F32),
            pltpu.VMEM((heads, 2, tokens, 2 * DK), BF16),
            pltpu.VMEM((heads, 2, DK, tokens), BF16),
            pltpu.VMEM((heads, tokens, tokens), F32),
            pltpu.VMEM((heads, tokens, tokens), F32),
            pltpu.VMEM((heads, DK, tokens), F32),
            pltpu.VMEM((heads, tokens, DK), F32),
            pltpu.VMEM((heads, tokens, 2 * DK), F32),
            state(), state(), state(), state(), state(), state(),
            pltpu.VMEM((2, groups, tiles, 8, DK), F32),
            pltpu.VMEM((2, groups, nz, tiles, 8, DK), F32),
            pltpu.VMEM((tiles, 8, DK), F32),
            pltpu.VMEM((tokens, width // 2), F32),
            pltpu.VMEM((tokens, width // 2), F32),
            pltpu.VMEM((width // 2, 2 * tokens), BF16),
            pltpu.VMEM((groups, 2 * tokens, wide), BF16),
            pltpu.VMEM((groups, tokens, wide), F32),
            pltpu.VMEM((groups, tokens, wide), F32),
            pltpu.VMEM((groups, nx, nz, ny, rows, wide), F32),
        ]
        count = {"x": nx, "z": nz, "y": ny}
        for order, rws, lns in scatter_parts(rows):
            cut = halved(order, count)
            shape = tuple(count[a] // 2 if a == cut else count[a] for a in "xzy" if a != order[0])
            scratch.append(pltpu.VMEM((groups, 2) + shape + (rws.size, lns.size), F32))
            for n in range(3):
                slots = 2 if n == 0 and count[order[0]] == 4 else max(count[order[n]] - 1, 1)
                left = tuple(count[a] for a in "xzy" if a not in order[: n + 1])
                scratch.append(pltpu.VMEM((groups, slots) + left + (rws.size, lns.size), F32))
        scratch += [dma(3), dma(heads), dma(2), dma(2), dma(2, groups)]
        scratch += [dma(groups)] * 8 + [dma(2, groups, nz)] * 2 + [dma(3, 4, groups)] * 2
        any_space = pl.BlockSpec(memory_space=pl.ANY)
        vmem = pl.BlockSpec(memory_space=pltpu.VMEM)
        smem = pl.BlockSpec(memory_space=pltpu.SMEM)
        return pl.pallas_call(
            functools.partial(mesa_kernel, (nx, nz, ny, heads, tokens, width)),
            out_shape=(
                jax.ShapeDtypeStruct((1, tokens, width), BF16),
                jax.ShapeDtypeStruct((1, tokens, heads * DK), F32),
                jax.ShapeDtypeStruct((rows, heads * DK), F32),
                jax.ShapeDtypeStruct((rows, heads * DK), F32),
            ),
            in_specs=[any_space, any_space, vmem, smem, any_space, any_space, any_space, smem],
            out_specs=(vmem, vmem, vmem, vmem),
            scratch_shapes=scratch,
            compiler_params=pltpu.CompilerParams(
                collective_id=0, has_side_effects=True, vmem_limit_bytes=63 << 20
            ),
            name="mesa_backward",
        )(layer_input, queries, jnp.swapaxes(gates, 1, 2), regularizer, key_weight, value_weight, out_cotangent, lengths)

    in_specs = (
        P("dp", "ctx", None),
        P("dp", "ctx", None),
        P("dp", "ctx", None),
        P(),
        P(),
        P(),
        P("dp", "ctx", None),
        P("dp", "ctx"),
    )
    out_specs = (
        P("dp", "ctx", None),
        P("dp", "ctx", None),
        P(("dp", "ctx"), None),
        P(("dp", "ctx"), None),
    )
    return jax.shard_map(body, mesh=mesh, in_specs=in_specs, out_specs=out_specs, check_vma=False)
```

```python
import functools

import jax
import jax.numpy as jnp
from jax import lax
from jax.experimental import pallas as pl
from jax.experimental.pallas import tpu as pltpu
from jax.sharding import PartitionSpec as P

ITERS = 4
TINY = 1e-06
DK = 128
PAIR = 2
F32 = jnp.float32
BF16 = jnp.bfloat16
MESH = pl.DeviceIdType.MESH


def split(a):
    high = a.astype(BF16)
    return high, (a - high.astype(F32)).astype(BF16)


def dot(a, b):
    return jnp.dot(a, b, preferred_element_type=F32)


def left3(parts):
    high, low = parts
    return jnp.concatenate([high, low, high], axis=1)


def right3(parts):
    high, low = parts
    return jnp.concatenate([high, high, low], axis=0)


def dot3(a, b):
    return dot(left3(a), right3(b))


def pack(sym):
    half = DK // 2
    row = lax.broadcasted_iota(jnp.int32, (half, DK), 0)
    lane = lax.broadcasted_iota(jnp.int32, (half, DK), 1)
    low = pltpu.roll(sym[half:], half, 1)
    diag = jnp.sum(jnp.where(lane == row, low, 0.0), axis=0, keepdims=True)
    return jnp.where(lane < row, low, sym[0:half]), diag


def unpack(packed, diag):
    half = DK // 2
    row = lax.broadcasted_iota(jnp.int32, (half, DK), 0)
    lane = lax.broadcasted_iota(jnp.int32, (half, DK), 1)
    diag = pltpu.roll(jnp.broadcast_to(diag, (half, DK)), half, 1)
    upper = jnp.where(lane > row, packed, 0.0)
    lower = pltpu.roll(jnp.where(lane < row, packed, 0.0), half, 1)
    off = jnp.concatenate([upper, lower], axis=0)
    on = jnp.concatenate(
        [jnp.where(lane == row, packed, 0.0), jnp.where(lane == row + half, diag, 0.0)], axis=0
    )
    return off + off.T + on


def mesa_kernel(
    sizes,
    x_ref, q_ref, gates_ref, reg_ref, wk_ref, wv_ref, g_ref, len_ref,
    ig_ref, qg_ref, kwg_ref, vwg_ref,
    x_s, w_s, q_s, g_s, ig_s, qg_s, run_s, tot_s, sw_s, ew_s, fac_snd, fac_rcv,
    kv_s, kt_s, dt_s, vs_s, rhs_s, ewc_s, loc_s,
    snd1, rcv1, rcv2, snd3, rcv3, rcv4, tot_snd, tot_rcv, carry_s,
    xs_snd, xs_rcv, xt_s, gr_s, sib_snd, sib_rcv,
    wa, ra0, ra1, ra2, ra3, wb, rb0, rb1, rb2, rb3, wc, rc0, rc1, rc2, rc3,
    out_sem, ld_sem, w_sem, fac_sem, x_sem, sib_sem, s1, r1, s2, r2, s3, r3, s4, r4, ts, tr, rs_snd, rs_rcv,
):
    nx, nz, ny, heads, tokens, width = sizes
    nctx = nz * ny
    groups = heads // PAIR
    per = 24 // ny
    gram_rows, pair_rows = DK // 2 // ny, DK // ny
    xb = width // (2 * nx)
    rows = xb // nctx
    half = rows // 2
    dp, ctx = lax.axis_index("dp"), lax.axis_index("ctx")
    mx, mc = lax.div(dp, 2), lax.rem(dp, 2)
    mz, my = lax.div(ctx, ny), lax.rem(ctx, ny)
    sib = mx * 2 + (1 - mc)

    barrier = pltpu.get_barrier_semaphore()
    for o in range(1, nctx):
        pl.semaphore_signal(barrier, inc=1, device_id=(dp, lax.rem(ctx + o, nctx)), device_id_type=MESH)
    pl.semaphore_signal(barrier, inc=1, device_id=(sib, ctx), device_id_type=MESH)
    for o in range(1, nx):
        pl.semaphore_signal(
            barrier, inc=1, device_id=(lax.rem(mx + o, nx) * 2 + mc, ctx), device_id_type=MESH
        )

    pltpu.make_async_copy(x_ref.at[0], x_s, ld_sem.at[0]).start()
    def load_weights(h):
        cols = pl.ds(h * DK, DK)
        pltpu.make_async_copy(wk_ref.at[:, cols], w_s.at[h, :, pl.ds(0, DK)], w_sem.at[h]).start()
        pltpu.make_async_copy(wv_ref.at[:, cols], w_s.at[h, :, pl.ds(DK, DK)], w_sem.at[h]).start()

    for h in range(heads):
        load_weights(h)
    for h in range(heads):
        cols = pl.ds(h * DK, DK)
        pltpu.make_async_copy(g_ref.at[0, :, cols], g_s.at[h], ld_sem.at[1]).start()
        pltpu.make_async_copy(q_ref.at[0, :, cols], q_s.at[h], ld_sem.at[2]).start()

    length = len_ref[0, 0]
    run = jnp.log(gates_ref[0])
    lane = lax.broadcasted_iota(jnp.int32, (heads, tokens), 1)
    step = 1
    while step < tokens:
        run = run + jnp.where(lane >= step, pltpu.roll(run, step, 1), 0.0)
        step *= 2
    total = jnp.broadcast_to(run[:, tokens - 1 : tokens], (heads, tokens))
    run_s[...] = run
    tot_s[...] = total
    sw_s[...] = jnp.exp(run)
    ew_s[...] = jnp.exp(total - run)
    fac_snd[...] = jnp.exp(total[:, 0:DK])

    mask_rows = (lax.broadcasted_iota(jnp.int32, (tokens, 2 * DK), 0) < length).astype(F32)
    mask_lane = (lax.broadcasted_iota(jnp.int32, (1, tokens), 1) < length).astype(F32)

    def across_y(src, dst, g, send, recv):
        for o in range(1, ny):
            to = lax.rem(my + o, ny)
            pltpu.make_async_remote_copy(
                src_ref=src.at[g, to], dst_ref=dst.at[g, my], send_sem=send.at[g], recv_sem=recv.at[g],
                device_id=(dp, mz * ny + to), device_id_type=MESH,
            ).start()
        dst[g, my] = src[g, my]

    def wait_all(buf, sem):
        pltpu.make_async_copy(buf, buf, sem).wait()

    def wait_others(buf, g, sem):
        wait_all(buf.at[g, pl.ds(0, ny - 1)], sem.at[g])

    def wait_sent(buf, g, sem):
        part = buf.at[g, pl.ds(0, ny - 1)]
        pltpu.make_async_copy(part, part, sem.at[g]).wait()

    def store_state(buf, g, grams, pairs):
        head = lax.broadcasted_iota(jnp.int32, (heads, DK), 0)
        diags = jnp.zeros((heads, DK), F32)
        for i in range(PAIR):
            packed, diag = pack(grams[i])
            diags = jnp.where(head == g * PAIR + i, diag, diags)
            for to in range(ny):
                buf[g, to, i * per : i * per + per // 3] = packed[
                    to * gram_rows : (to + 1) * gram_rows
                ].reshape(per // 3, 8, DK)
                buf[g, to, i * per + per // 3 : (i + 1) * per] = pairs[i][
                    to * pair_rows : (to + 1) * pair_rows
                ].reshape(2 * per // 3, 8, DK)
        for to in range(ny):
            buf[g, to, PAIR * per] = diags

    def load_state(buf, g, i):
        head = lax.broadcasted_iota(jnp.int32, (heads, DK), 0)
        diag = jnp.sum(jnp.where(head == g * PAIR + i, buf[g, 0, PAIR * per], 0.0), axis=0, keepdims=True)
        packed = jnp.concatenate(
            [buf[g, at, i * per : i * per + per // 3].reshape(gram_rows, DK) for at in range(ny)], axis=0
        )
        pair = jnp.concatenate(
            [buf[g, at, i * per + per // 3 : (i + 1) * per].reshape(pair_rows, DK) for at in range(ny)],
            axis=0,
        )
        return unpack(packed, diag), pair

    def factors(c, g):
        return [fac_rcv[c, pl.ds(g * PAIR + i, 1), :] for i in range(PAIR)] + [fac_rcv[c]]

    def decayed(factor, tiles):
        scaled = [tiles[i * per : (i + 1) * per] * factor[i] for i in range(PAIR)]
        return jnp.concatenate(scaled + [tiles[PAIR * per :] * factor[PAIR]], axis=0)

    def project(g):
        grams, pairs = [], []
        for i in range(PAIR):
            h = g * PAIR + i
            wait_all(w_s.at[h], w_sem.at[h])
            kv = dot(x_s[...], w_s[h]) * mask_rows
            parts = split(kv)
            kv_s[h, 0], kv_s[h, 1] = parts
            kt = kv[:, 0:DK].T
            kt_s[h, 0], kt_s[h, 1] = split(kt)
            state = dot3(split(kt * ew_s[pl.ds(h, 1), :]), parts)
            grams.append(state[:, 0:DK])
            pairs.append(state[:, DK:])
        store_state(snd1, g, grams, pairs)

    def tables(g):
        for i in range(PAIR):
            h = g * PAIR + i
            run_row = run_s[pl.ds(h, 1), :]
            run_col = jnp.broadcast_to(run_row, (DK, tokens)).T
            ewc_s[h] = jnp.exp(tot_s[pl.ds(h, 1), :][:, 0:DK] - run_col)
            gap = run_row - jnp.concatenate([run_col] * (tokens // DK), axis=1)
            later = lax.broadcasted_iota(jnp.int32, (tokens, tokens), 1) >= lax.broadcasted_iota(
                jnp.int32, (tokens, tokens), 0
            )
            table = jnp.exp(jnp.where(later, gap, -1e30))
            dt_s[h] = table
            gt = ((g_s[h].astype(F32)).T * mask_lane).astype(BF16)
            v_both = jnp.concatenate([kv_s[h, 0, :, DK:], kv_s[h, 1, :, DK:]], axis=1)
            scores = dot(v_both, jnp.concatenate([gt, gt], axis=0)) * table
            vs_s[h] = scores
            rhs_s[h] = dot3((kt_s[h, 0], kt_s[h, 1]), split(scores))

    def prefix_y(buf, g, back):
        held = None
        for at in reversed(range(ny)) if back else range(ny):
            mine = buf[g, at]
            if held is None:
                buf[g, at] = jnp.zeros_like(mine)
                held = mine
            else:
                buf[g, at] = held
                held = decayed(factors(mz * ny + at, g), held) + mine
        tot_snd[back, g] = held
        for o in range(1, nz):
            to = lax.rem(mz + o, nz)

            @pl.when(to < mz if back else to > mz)
            def _():
                total_copy(back, g, to).start()

    def total_copy(back, g, to):
        return pltpu.make_async_remote_copy(
            src_ref=tot_snd.at[back, g], dst_ref=tot_rcv.at[back, g, mz],
            send_sem=ts.at[back, g, to], recv_sem=tr.at[back, g, mz],
            device_id=(dp, to * ny + my), device_id_type=MESH,
        )

    def prefix_z(buf, g, back):
        carry_s[...] = jnp.zeros_like(carry_s)
        for at in reversed(range(nz)) if back else range(nz):

            @pl.when(at > mz if back else at < mz)
            def _():
                wait_all(tot_rcv.at[back, g, at], tr.at[back, g, at])
                factor = factors(at * ny, g)
                for y in range(1, ny):
                    factor = [a * b for a, b in zip(factor, factors(at * ny + y, g))]
                carry_s[...] = decayed(factor, carry_s[...]) + tot_rcv[back, g, at]

        carried = carry_s[...]
        for at in reversed(range(ny)) if back else range(ny):
            buf[g, at] = buf[g, at] + carried
            carried = decayed(factors(mz * ny + at, g), carried)

    def solve(g, between):
        state = [load_state(rcv2, g, i) for i in range(PAIR)]
        x, r, p, rr, keys, kts, big, gts = ([None] * PAIR for _ in range(8))
        for i in range(PAIR):
            h = g * PAIR + i
            qt = q_s[h].astype(F32).T
            gts[i] = ((g_s[h].astype(F32)).T * mask_lane).astype(BF16)
            gram, pair = split(state[i][0]), split(state[i][1])
            right = rhs_s[h] + sw_s[pl.ds(h, 1), :] * dot(
                jnp.concatenate(pair, axis=1), jnp.concatenate([gts[i], gts[i]], axis=0)
            )
            p[i] = r[i] = jnp.concatenate([qt, right], axis=1)
            rr[i] = jnp.sum(r[i] * r[i], axis=0, keepdims=True)
            keys[i] = (kv_s[h, 0, :, 0:DK], kv_s[h, 1, :, 0:DK])
            kts[i] = (kt_s[h, 0], kt_s[h, 1])
            big[i] = tuple(jnp.concatenate([a, b], axis=0) for a, b in zip(keys[i], gram))
        for it in range(ITERS):
            last = it == ITERS - 1
            for i in range(PAIR):
                h = g * PAIR + i
                table = jnp.concatenate([dt_s[h]] * 2, axis=1)
                sw = jnp.concatenate([sw_s[pl.ds(h, 1), :]] * 2, axis=1)
                if last:
                    both = dot(big[i][0], p[i].astype(BF16))
                    inner = dot(kts[i][0], (both[0:tokens] * table).astype(BF16))
                else:
                    both = dot3(big[i], split(p[i]))
                    inner = dot3(kts[i], split(both[0:tokens] * table))
                image = reg_ref[h] * p[i] + sw * both[tokens:] + inner
                size = rr[i] / (jnp.sum(p[i] * image, axis=0, keepdims=True) + TINY)
                x[i] = size * p[i] if it == 0 else x[i] + size * p[i]
                if not last:
                    r[i] = r[i] - size * image
                    following = jnp.sum(r[i] * r[i], axis=0, keepdims=True)
                    p[i] = r[i] + (following / (rr[i] + TINY)) * p[i]
                    rr[i] = following
            between[it]()
        grams, pairs = [], []
        for i in range(PAIR):
            h = g * PAIR + i
            xt, yt = x[i][:, 0:tokens], x[i][:, tokens:]
            xn, yn = xt.T, yt.T
            qg_s[:, pl.ds(pl.multiple_of(h * DK, DK), DK)] = yn
            gn = (g_s[h].astype(F32) * mask_rows[:, 0:DK]).astype(BF16)
            y_high, y_low = split(yn)
            yg = (
                jnp.concatenate([y_high, gn], axis=1),
                jnp.concatenate([y_low, jnp.zeros_like(gn)], axis=1),
            )
            back = dot3(split(xt * sw_s[pl.ds(h, 1), :]), yg)
            grams.append(-(back[:, 0:DK] + back[:, 0:DK].T))
            pairs.append(back[:, DK:])
            table = jnp.concatenate([dt_s[h]] * 2, axis=1)
            scores = dot3(keys[i], split(x[i])) * table
            sol, adj = scores[:, 0:tokens], scores[:, tokens:]
            from_x = dot3(split(vs_s[h] - adj), split(xn))
            from_yg = dot3(split(sol), yg)
            loc_s[h] = jnp.concatenate([from_x - from_yg[:, 0:DK], from_yg[:, DK:]], axis=1)
        store_state(snd3, g, grams, pairs)

    def gradients(g):
        for i in range(PAIR):
            h = g * PAIR + i
            sym, pair_t = load_state(rcv4, g, i)
            pair = pair_t.T
            both = jnp.concatenate(
                [
                    jnp.concatenate([sym, pair_t], axis=1),
                    jnp.concatenate([pair, jnp.zeros_like(pair)], axis=1),
                ],
                axis=0,
            )
            carried = dot3((kv_s[h, 0], kv_s[h, 1]), split(both))
            decay = jnp.concatenate([ewc_s[h]] * 2, axis=1)
            grad = ((loc_s[h] + decay * carried) * mask_rows).astype(BF16)
            gr_s[g, 0:tokens, pl.ds(i * 2 * DK, 2 * DK)] = grad
            sib_snd[g, :, pl.ds(i * 2 * DK, 2 * DK)] = grad.astype(F32)

    def sib_copy(g):
        return pltpu.make_async_remote_copy(
            src_ref=sib_snd.at[g], dst_ref=sib_rcv.at[g], send_sem=sib_sem.at[0, g], recv_sem=sib_sem.at[1, g],
            device_id=(sib, ctx), device_id_type=MESH,
        )

    me = {"x": mx, "z": mz, "y": my}
    count = {"x": nx, "z": nz, "y": ny}
    whole = (wa, wb, wc)
    parts = [
        (order, rws, lns, bufs)
        for (order, rws, lns), bufs in zip(
            scatter_parts(rows), ((ra0, ra1, ra2, ra3), (rb0, rb1, rb2, rb3), (rc0, rc1, rc2, rc3))
        )
    ]

    def device(axis, at):
        place = dict(me)
        place[axis] = at
        return (place["x"] * 2 + mc, place["z"] * ny + place["y"])

    def chunk(n, part, g, at, side=None):
        order, rws, lns, bufs = parts[part]
        spot = (at,)
        if side is not None:
            half_count = count[order[1]] // 2
            spot = (at, pl.ds(side * half_count, half_count))
        if n == 0:
            return whole[part].at[(g,) + spot]
        return bufs[n].at[(g, 0) + spot]

    def send(src, dst, part, n, g, axis, to):
        pltpu.make_async_remote_copy(
            src_ref=src, dst_ref=dst, send_sem=rs_snd.at[part, n, g], recv_sem=rs_rcv.at[part, n, g],
            device_id=device(axis, to), device_id_type=MESH,
        ).start()

    def sides(axis):
        return lax.rem(me[axis] + 1, count[axis]), lax.rem(me[axis] + count[axis] - 1, count[axis])

    def scatter_far(g):
        for part, (order, rws, lns, bufs) in enumerate(parts):
            axis = order[0]
            if count[axis] == 4:
                for side, to in enumerate(sides(axis)):
                    far = lax.rem(me[axis] + 2, 4)
                    send(chunk(0, part, g, far, side), bufs[0].at[g, side], part, 0, g, axis, to)

    def scatter_near(g):
        for part, (order, rws, lns, bufs) in enumerate(parts):
            axis = order[0]
            if count[axis] == 4:
                wait_all(bufs[0].at[g], rs_rcv.at[part, 0, g])
                for side, to in enumerate(sides(axis)):
                    half_ref = chunk(0, part, g, to, side)
                    half_ref[...] = half_ref[...] + bufs[0][g, side]
                    send(chunk(0, part, g, to), bufs[1].at[g, side], part, 1, g, axis, to)
            else:
                scatter_direct(0, part, g)

    def scatter_direct(n, part, g):
        order, rws, lns, bufs = parts[part]
        axis = order[n]
        for o in range(1, count[axis]):
            to = lax.rem(me[axis] + o, count[axis])
            send(chunk(n, part, g, to), bufs[n + 1].at[g, o - 1], part, n + 1, g, axis, to)

    def scatter_start(n, g):
        for part in range(3):
            scatter_direct(n, part, g)

    def scatter_add(n, g):
        for part, (order, rws, lns, bufs) in enumerate(parts):
            summed = chunk(n, part, g, me[order[n]])[...]
            if count[order[n]] > 1:
                wait_all(bufs[n + 1].at[g], rs_rcv.at[part, n + 1, g])
                for o in range(bufs[n + 1].shape[1]):
                    summed = summed + bufs[n + 1][g, o]
            if n < 2:
                bufs[n + 1][g, 0] = summed
            else:
                first, second = (pl.ds((g * PAIR + i) * DK, DK) for i in range(PAIR))
                if part < 2:
                    kwg_ref[rws, first] = summed[:, 0:DK]
                    vwg_ref[rws, first] = summed[:, DK : 2 * DK]
                    kwg_ref[rws, second] = summed[:, 2 * DK :]
                else:
                    vwg_ref[rws, second] = summed

    def weight_part(g):
        sib_copy(g).wait_recv()
        gr_s[g, tokens:, :] = sib_rcv[g].astype(BF16)
        for k in range(nx):
            out = dot(xt_s[k * xb : (k + 1) * xb, :], gr_s[g])
            out = out.reshape(nz, ny, rows, PAIR * 2 * DK)
            for part, (order, rws, lns, bufs) in enumerate(parts):
                for z in range(nz):
                    for y in range(ny):
                        place = {"x": k, "z": z, "y": y}
                        whole[part][(g,) + tuple(place[a] for a in order)] = out[
                            z, y, rws.start : rws.start + rws.size, lns.start : lns.start + lns.size
                        ]
        scatter_far(g)

    def input_gradient():
        def columns(n, carry):
            span = pl.ds(pl.multiple_of(n * 256, 256), 256)
            total = None
            for h in range(heads):
                grad = gr_s[h // PAIR, 0:tokens, (h % PAIR) * 2 * DK : (h % PAIR + 1) * 2 * DK]
                term = lax.dot_general(
                    grad, w_s[h, span, :], (((1,), (1,)), ((), ())), preferred_element_type=F32
                )
                total = term if total is None else total + term
            ig_s[:, span] = total.astype(BF16)
            return carry

        lax.fori_loop(0, width // 256, columns, 0)

    def forward_y(g):
        wait_others(rcv1, g, r1)
        prefix_y(rcv1, g, 0)

    def forward_z(g):
        prefix_z(rcv1, g, 0)
        across_y(rcv1, rcv2, g, s2, r2)

    def backward_y(g):
        wait_others(rcv3, g, r3)
        prefix_y(rcv3, g, 1)

    def backward_z(g):
        prefix_z(rcv3, g, 1)
        across_y(rcv3, rcv4, g, s4, r4)

    def backward_grads(g):
        wait_others(rcv4, g, r4)
        gradients(g)
        sib_copy(g).start()

    def reduce_two(g):
        scatter_add(0, g)
        scatter_start(1, g)

    def reduce_three(g):
        scatter_add(1, g)
        scatter_start(2, g)

    def reduce_last(g):
        scatter_add(2, g)

    def send_state(g):
        across_y(snd1, rcv1, g, s1, r1)

    wait_all(x_s, ld_sem.at[0])
    project(0)
    pl.semaphore_wait(barrier, nctx - 1 + 1 + nx - 1)
    send_state(0)
    for o in range(1, nctx):
        to = lax.rem(ctx + o, nctx)
        pltpu.make_async_remote_copy(
            src_ref=fac_snd, dst_ref=fac_rcv.at[ctx], send_sem=fac_sem.at[0], recv_sem=fac_sem.at[1],
            device_id=(dp, to), device_id_type=MESH,
        ).start()
    fac_rcv[ctx] = fac_snd[...]
    project(1)
    send_state(1)
    wait_all(g_s, ld_sem.at[1])
    wait_all(q_s, ld_sem.at[2])
    tables(0)
    tables(1)
    wait_all(fac_rcv.at[pl.ds(0, nctx - 1)], fac_sem.at[1])
    forward_y(0)
    project(2)
    forward_y(1)
    forward_z(0)
    send_state(2)
    forward_z(1)
    for k in range(nx):
        theirs = pl.ds(pl.multiple_of(k * 2 * xb + (1 - mc) * xb, xb), xb)
        xs_snd[:, k * xb : (k + 1) * xb] = x_s[:, theirs].astype(F32)
    x_copy = pltpu.make_async_remote_copy(
        src_ref=xs_snd, dst_ref=xs_rcv, send_sem=x_sem.at[0], recv_sem=x_sem.at[1],
        device_id=(sib, ctx), device_id_type=MESH,
    )
    x_copy.start()
    project(3)
    send_state(3)
    tables(2)
    tables(3)
    forward_y(2)
    for k in range(nx):
        mine = pl.ds(pl.multiple_of(k * 2 * xb + mc * xb, xb), xb)
        xt_s[k * xb : (k + 1) * xb, 0:tokens] = x_s[:, mine].astype(F32).T.astype(BF16)

    def during(s, first, fn, count=groups):
        @pl.when(jnp.logical_and(s >= first, s < first + count))
        def _():
            fn(s - first)

    def with_solve(s, carry):
        def zero():
            during(s, 3, weight_part)
            pl.when(s == 0)(lambda: forward_z(2))

        def one():
            pl.when(s == 0)(lambda: forward_y(3))
            during(s, 2, backward_z)

        def two():
            pl.when(s == 0)(lambda: forward_z(3))

        def three():
            during(s, 1, backward_y)
            during(s, 3, scatter_near)

        wait_others(rcv2, s, r2)
        solve(s, (zero, one, two, three))
        across_y(snd3, rcv3, s, s3, r3)
        during(s, 2, backward_grads)

        @pl.when(s == 0)
        def _():
            x_copy.wait_recv()
            for k in range(nx):
                xt_s[k * xb : (k + 1) * xb, tokens:] = xs_rcv[:, k * xb : (k + 1) * xb].T.astype(BF16)

        return carry

    lax.fori_loop(0, groups, with_solve, 0)
    qg_copy = pltpu.make_async_copy(qg_s, qg_ref.at[0], out_sem.at[0])
    qg_copy.start()
    backward_z(2)
    weight_part(1)
    backward_y(3)
    backward_grads(2)
    scatter_near(1)
    backward_z(3)
    weight_part(2)
    reduce_two(0)
    backward_grads(3)
    scatter_near(2)
    weight_part(3)
    reduce_two(1)
    reduce_three(0)
    input_gradient()
    ig_copy = pltpu.make_async_copy(ig_s, ig_ref.at[0], out_sem.at[1])
    ig_copy.start()
    scatter_near(3)
    reduce_two(2)
    reduce_three(1)
    reduce_last(0)
    reduce_two(3)
    reduce_three(2)
    reduce_last(1)
    reduce_three(3)
    reduce_last(2)
    reduce_last(3)

    qg_copy.wait()
    ig_copy.wait()
    sent = pltpu.make_async_copy(
        fac_rcv.at[pl.ds(0, nctx - 1)], fac_rcv.at[pl.ds(0, nctx - 1)], fac_sem.at[0]
    )
    sent.wait()
    x_copy.wait_send()

    def drain(g, carry):
        wait_sent(snd1, g, s1)
        wait_sent(rcv1, g, s2)
        wait_sent(snd3, g, s3)
        wait_sent(rcv3, g, s4)
        sib_copy(g).wait_send()
        for part, (order, rws, lns, bufs) in enumerate(parts):
            for n in range(4):
                if count[order[max(n - 1, 0)]] > 1 and (n > 0 or count[order[0]] == 4):
                    wait_all(bufs[n].at[g], rs_snd.at[part, n, g])
        for back in range(2):
            for o in range(1, nz):
                to = lax.rem(mz + o, nz)

                @pl.when(to < mz if back else to > mz)
                def _():
                    total_copy(back, g, to).wait_send()

        return carry

    lax.fori_loop(0, groups, drain, 0)


def copy_kernel(a, b, c, d, a_out, b_out, c_out, d_out):
    for src, dst in ((a, a_out), (b, b_out), (c, c_out), (d, d_out)):
        dst[...] = src[...]


def copied(arrays):
    steps = 2
    specs = [
        pl.BlockSpec((1, a.shape[1] // steps, a.shape[2]), lambda i: (0, i, 0))
        if len(a.shape) == 3
        else pl.BlockSpec((a.shape[0] // steps, a.shape[1]), lambda i: (i, 0))
        for a in arrays
    ]
    return pl.pallas_call(
        copy_kernel,
        out_shape=tuple(jax.ShapeDtypeStruct(a.shape, a.dtype) for a in arrays),
        grid=(steps,),
        in_specs=specs,
        out_specs=tuple(specs),
        compiler_params=pltpu.CompilerParams(vmem_limit_bytes=62 << 20),
        name="results",
    )(*arrays)


def scatter_parts(rows):
    return (
        ("xyz", pl.ds(0, rows // 2), pl.ds(0, 3 * DK)),
        ("zxy", pl.ds(rows // 2, rows // 2), pl.ds(0, 3 * DK)),
        ("yzx", pl.ds(0, rows), pl.ds(3 * DK, DK)),
    )


def solution(mesh):
    nx = mesh.shape["dp"] // 2
    nctx = mesh.shape["ctx"]
    ny = min(nctx, 4)
    nz = nctx // ny

    def body(layer_input, queries, gates, regularizer, key_weight, value_weight, out_cotangent, lengths):
        tokens, width = layer_input.shape[1:]
        heads = gates.shape[2]
        groups = heads // PAIR
        rows = width // (2 * nx * nctx)
        tiles = PAIR * 24 // ny + 1
        wide = PAIR * 2 * DK
        state = lambda: pltpu.VMEM((groups, ny, tiles, 8, DK), F32)
        dma = lambda *shape: pltpu.SemaphoreType.DMA(shape)
        scratch = [
            pltpu.VMEM((tokens, width), BF16),
            pltpu.VMEM((heads, width, 2 * DK), BF16),
            pltpu.VMEM((heads, tokens, DK), BF16),
            pltpu.VMEM((heads, tokens, DK), BF16),
            pltpu.VMEM((tokens, width), BF16),
            pltpu.VMEM((tokens, heads * DK), F32),
            pltpu.VMEM((heads, tokens), F32),
            pltpu.VMEM((heads, tokens), F32),
            pltpu.VMEM((heads, tokens), F32),
            pltpu.VMEM((heads, tokens), F32),
            pltpu.VMEM((heads, DK), F32),
            pltpu.VMEM((nctx, heads, DK), F32),
            pltpu.VMEM((heads, 2, tokens, 2 * DK), BF16),
            pltpu.VMEM((heads, 2, DK, tokens), BF16),
            pltpu.VMEM((heads, tokens, tokens), F32),
            pltpu.VMEM((heads, tokens, tokens), F32),
            pltpu.VMEM((heads, DK, tokens), F32),
            pltpu.VMEM((heads, tokens, DK), F32),
            pltpu.VMEM((heads, tokens, 2 * DK), F32),
            state(), state(), state(), state(), state(), state(),
            pltpu.VMEM((2, groups, tiles, 8, DK), F32),
            pltpu.VMEM((2, groups, nz, tiles, 8, DK), F32),
            pltpu.VMEM((tiles, 8, DK), F32),
            pltpu.VMEM((tokens, width // 2), F32),
            pltpu.VMEM((tokens, width // 2), F32),
            pltpu.VMEM((width // 2, 2 * tokens), BF16),
            pltpu.VMEM((groups, 2 * tokens, wide), BF16),
            pltpu.VMEM((groups, tokens, wide), F32),
            pltpu.VMEM((groups, tokens, wide), F32),
        ]
        count = {"x": nx, "z": nz, "y": ny}
        for order, rws, lns in scatter_parts(rows):
            a, b, c = (count[axis] for axis in order)
            scratch.append(pltpu.VMEM((groups, a, b, c, rws.size, lns.size), F32))
            scratch.append(pltpu.VMEM((groups, 2, max(b // 2, 1), c, rws.size, lns.size), F32))
            for n in range(3):
                slots = 2 if n == 0 and count[order[0]] == 4 else max(count[order[n]] - 1, 1)
                left = tuple(count[a] for a in order[n + 1 :])
                scratch.append(pltpu.VMEM((groups, slots) + left + (rws.size, lns.size), F32))
        scratch += [dma(2), dma(3), dma(heads), dma(2), dma(2), dma(2, groups)]
        scratch += [dma(groups)] * 8 + [dma(2, groups, nz)] * 2 + [dma(3, 4, groups)] * 2
        any_space = pl.BlockSpec(memory_space=pl.ANY)
        vmem = pl.BlockSpec(memory_space=pltpu.VMEM)
        smem = pl.BlockSpec(memory_space=pltpu.SMEM)
        results = pl.pallas_call(
            functools.partial(mesa_kernel, (nx, nz, ny, heads, tokens, width)),
            out_shape=(
                jax.ShapeDtypeStruct((1, tokens, width), BF16),
                jax.ShapeDtypeStruct((1, tokens, heads * DK), F32),
                jax.ShapeDtypeStruct((rows, heads * DK), F32),
                jax.ShapeDtypeStruct((rows, heads * DK), F32),
            ),
            in_specs=[any_space, any_space, vmem, smem, any_space, any_space, any_space, smem],
            out_specs=(any_space, any_space, vmem, vmem),
            scratch_shapes=scratch,
            compiler_params=pltpu.CompilerParams(
                collective_id=0, has_side_effects=True, vmem_limit_bytes=63 << 20
            ),
            name="mesa_backward",
        )(layer_input, queries, jnp.swapaxes(gates, 1, 2), regularizer, key_weight, value_weight, out_cotangent, lengths)
        return copied(results)

    in_specs = (
        P("dp", "ctx", None),
        P("dp", "ctx", None),
        P("dp", "ctx", None),
        P(),
        P(),
        P(),
        P("dp", "ctx", None),
        P("dp", "ctx"),
    )
    out_specs = (
        P("dp", "ctx", None),
        P("dp", "ctx", None),
        P(("dp", "ctx"), None),
        P(("dp", "ctx"), None),
    )
    return jax.shard_map(body, mesh=mesh, in_specs=in_specs, out_specs=out_specs, check_vma=False)
```

```python
import functools

import jax
import jax.numpy as jnp
from jax import lax
from jax.experimental import pallas as pl
from jax.experimental.pallas import tpu as pltpu
from jax.sharding import PartitionSpec as P

ITERS = 4
TINY = 1e-06
DK = 128
PAIR = 2
F32 = jnp.float32
BF16 = jnp.bfloat16
MESH = pl.DeviceIdType.MESH


def split(a):
    high = a.astype(BF16)
    return high, (a - high.astype(F32)).astype(BF16)


def dot(a, b):
    return jnp.dot(a, b, preferred_element_type=F32)


def left3(parts):
    high, low = parts
    return jnp.concatenate([high, low, high], axis=1)


def right3(parts):
    high, low = parts
    return jnp.concatenate([high, high, low], axis=0)


def dot3(a, b):
    return dot(left3(a), right3(b))


def pack(sym):
    half = DK // 2
    row = lax.broadcasted_iota(jnp.int32, (half, DK), 0)
    lane = lax.broadcasted_iota(jnp.int32, (half, DK), 1)
    low = pltpu.roll(sym[half:], half, 1)
    diag = jnp.sum(jnp.where(lane == row, low, 0.0), axis=0, keepdims=True)
    return jnp.where(lane < row, low, sym[0:half]), diag


def unpack(packed, diag):
    half = DK // 2
    row = lax.broadcasted_iota(jnp.int32, (half, DK), 0)
    lane = lax.broadcasted_iota(jnp.int32, (half, DK), 1)
    diag = pltpu.roll(jnp.broadcast_to(diag, (half, DK)), half, 1)
    upper = jnp.where(lane > row, packed, 0.0)
    lower = pltpu.roll(jnp.where(lane < row, packed, 0.0), half, 1)
    off = jnp.concatenate([upper, lower], axis=0)
    on = jnp.concatenate(
        [jnp.where(lane == row, packed, 0.0), jnp.where(lane == row + half, diag, 0.0)], axis=0
    )
    return off + off.T + on


def mesa_kernel(
    sizes,
    x_ref, q_ref, gates_ref, reg_ref, wk_ref, wv_ref, g_ref, len_ref,
    ig_ref, qg_ref, kwg_ref, vwg_ref,
    x_s, w_s, q_s, g_s, ig_s, qg_s, run_s, tot_s, sw_s, ew_s, fac_snd, fac_rcv,
    kv_s, kt_s, dt_s, vs_s, rhs_s, ewc_s, loc_s,
    snd1, rcv1, rcv2, snd3, rcv3, rcv4, tot_snd, tot_rcv, carry_s,
    xs_snd, xs_rcv, xt_s, gr_s, sib_snd, sib_rcv,
    wa, ra0, ra1, ra2, ra3, wb, rb0, rb1, rb2, rb3, wc, rc0, rc1, rc2, rc3,
    out_sem, ld_sem, w_sem, fac_sem, x_sem, sib_sem, s1, r1, s2, r2, s3, r3, s4, r4, ts, tr, rs_snd, rs_rcv,
):
    nx, nz, ny, heads, tokens, width = sizes
    nctx = nz * ny
    groups = heads // PAIR
    per = 24 // ny
    gram_rows, pair_rows = DK // 2 // ny, DK // ny
    xb = width // (2 * nx)
    rows = xb // nctx
    half = rows // 2
    dp, ctx = lax.axis_index("dp"), lax.axis_index("ctx")
    mx, mc = lax.div(dp, 2), lax.rem(dp, 2)
    mz, my = lax.div(ctx, ny), lax.rem(ctx, ny)
    sib = mx * 2 + (1 - mc)

    barrier = pltpu.get_barrier_semaphore()
    for o in range(1, nctx):
        pl.semaphore_signal(barrier, inc=1, device_id=(dp, lax.rem(ctx + o, nctx)), device_id_type=MESH)
    pl.semaphore_signal(barrier, inc=1, device_id=(sib, ctx), device_id_type=MESH)
    for o in range(1, nx):
        pl.semaphore_signal(
            barrier, inc=1, device_id=(lax.rem(mx + o, nx) * 2 + mc, ctx), device_id_type=MESH
        )

    pltpu.make_async_copy(x_ref.at[0], x_s, ld_sem.at[0]).start()
    def load_weights(h):
        cols = pl.ds(h * DK, DK)
        pltpu.make_async_copy(wk_ref.at[:, cols], w_s.at[h, :, pl.ds(0, DK)], w_sem.at[h]).start()
        pltpu.make_async_copy(wv_ref.at[:, cols], w_s.at[h, :, pl.ds(DK, DK)], w_sem.at[h]).start()

    for h in range(heads):
        load_weights(h)
    for h in range(heads):
        cols = pl.ds(h * DK, DK)
        pltpu.make_async_copy(g_ref.at[0, :, cols], g_s.at[h], ld_sem.at[1]).start()
        pltpu.make_async_copy(q_ref.at[0, :, cols], q_s.at[h], ld_sem.at[2]).start()

    length = len_ref[0, 0]
    run = jnp.log(gates_ref[0])
    lane = lax.broadcasted_iota(jnp.int32, (heads, tokens), 1)
    step = 1
    while step < tokens:
        run = run + jnp.where(lane >= step, pltpu.roll(run, step, 1), 0.0)
        step *= 2
    total = jnp.broadcast_to(run[:, tokens - 1 : tokens], (heads, tokens))
    run_s[...] = run
    tot_s[...] = total
    sw_s[...] = jnp.exp(run)
    ew_s[...] = jnp.exp(total - run)
    fac_snd[...] = jnp.exp(total[:, 0:DK])

    mask_rows = (lax.broadcasted_iota(jnp.int32, (tokens, 2 * DK), 0) < length).astype(F32)
    mask_lane = (lax.broadcasted_iota(jnp.int32, (1, tokens), 1) < length).astype(F32)

    def across_y(src, dst, g, send, recv):
        for o in sorted(range(1, ny), key=lambda o: -min(o, ny - o)):
            to = lax.rem(my + o, ny)
            pltpu.make_async_remote_copy(
                src_ref=src.at[g, to], dst_ref=dst.at[g, my], send_sem=send.at[g], recv_sem=recv.at[g],
                device_id=(dp, mz * ny + to), device_id_type=MESH,
            ).start()
        dst[g, my] = src[g, my]

    def wait_all(buf, sem):
        pltpu.make_async_copy(buf, buf, sem).wait()

    def wait_others(buf, g, sem):
        wait_all(buf.at[g, pl.ds(0, ny - 1)], sem.at[g])

    def wait_sent(buf, g, sem):
        part = buf.at[g, pl.ds(0, ny - 1)]
        pltpu.make_async_copy(part, part, sem.at[g]).wait()

    def store_state(buf, g, grams, pairs):
        head = lax.broadcasted_iota(jnp.int32, (heads, DK), 0)
        diags = jnp.zeros((heads, DK), F32)
        for i in range(PAIR):
            packed, diag = pack(grams[i])
            diags = jnp.where(head == g * PAIR + i, diag, diags)
            for to in range(ny):
                buf[g, to, i * per : i * per + per // 3] = packed[
                    to * gram_rows : (to + 1) * gram_rows
                ].reshape(per // 3, 8, DK)
                buf[g, to, i * per + per // 3 : (i + 1) * per] = pairs[i][
                    to * pair_rows : (to + 1) * pair_rows
                ].reshape(2 * per // 3, 8, DK)
        for to in range(ny):
            buf[g, to, PAIR * per] = diags

    def load_state(buf, g, i):
        head = lax.broadcasted_iota(jnp.int32, (heads, DK), 0)
        diag = jnp.sum(jnp.where(head == g * PAIR + i, buf[g, 0, PAIR * per], 0.0), axis=0, keepdims=True)
        packed = jnp.concatenate(
            [buf[g, at, i * per : i * per + per // 3].reshape(gram_rows, DK) for at in range(ny)], axis=0
        )
        pair = jnp.concatenate(
            [buf[g, at, i * per + per // 3 : (i + 1) * per].reshape(pair_rows, DK) for at in range(ny)],
            axis=0,
        )
        return unpack(packed, diag), pair

    def factors(c, g):
        return [fac_rcv[c, pl.ds(g * PAIR + i, 1), :] for i in range(PAIR)] + [fac_rcv[c]]

    def decayed(factor, tiles):
        scaled = [tiles[i * per : (i + 1) * per] * factor[i] for i in range(PAIR)]
        return jnp.concatenate(scaled + [tiles[PAIR * per :] * factor[PAIR]], axis=0)

    def project(g):
        grams, pairs = [], []
        for i in range(PAIR):
            h = g * PAIR + i
            wait_all(w_s.at[h], w_sem.at[h])
            kv = dot(x_s[...], w_s[h]) * mask_rows
            parts = split(kv)
            kv_s[h, 0], kv_s[h, 1] = parts
            kt = kv[:, 0:DK].T
            kt_s[h, 0], kt_s[h, 1] = split(kt)
            state = dot3(split(kt * ew_s[pl.ds(h, 1), :]), parts)
            grams.append(state[:, 0:DK])
            pairs.append(state[:, DK:])
        store_state(snd1, g, grams, pairs)

    def tables(g):
        for i in range(PAIR):
            h = g * PAIR + i
            run_row = run_s[pl.ds(h, 1), :]
            run_col = jnp.broadcast_to(run_row, (DK, tokens)).T
            ewc_s[h] = jnp.exp(tot_s[pl.ds(h, 1), :][:, 0:DK] - run_col)
            gap = run_row - jnp.concatenate([run_col] * (tokens // DK), axis=1)
            later = lax.broadcasted_iota(jnp.int32, (tokens, tokens), 1) >= lax.broadcasted_iota(
                jnp.int32, (tokens, tokens), 0
            )
            table = jnp.exp(jnp.where(later, gap, -1e30))
            dt_s[h] = table
            gt = ((g_s[h].astype(F32)).T * mask_lane).astype(BF16)
            v_both = jnp.concatenate([kv_s[h, 0, :, DK:], kv_s[h, 1, :, DK:]], axis=1)
            scores = dot(v_both, jnp.concatenate([gt, gt], axis=0)) * table
            vs_s[h] = scores
            rhs_s[h] = dot3((kt_s[h, 0], kt_s[h, 1]), split(scores))

    def prefix_y(buf, g, back):
        held = None
        for at in reversed(range(ny)) if back else range(ny):
            mine = buf[g, at]
            if held is None:
                buf[g, at] = jnp.zeros_like(mine)
                held = mine
            else:
                buf[g, at] = held
                held = decayed(factors(mz * ny + at, g), held) + mine
        tot_snd[back, g] = held
        for o in range(1, nz):
            to = lax.rem(mz + o, nz)

            @pl.when(to < mz if back else to > mz)
            def _():
                total_copy(back, g, to).start()

    def total_copy(back, g, to):
        return pltpu.make_async_remote_copy(
            src_ref=tot_snd.at[back, g], dst_ref=tot_rcv.at[back, g, mz],
            send_sem=ts.at[back, g, to], recv_sem=tr.at[back, g, mz],
            device_id=(dp, to * ny + my), device_id_type=MESH,
        )

    def prefix_z(buf, g, back):
        carry_s[...] = jnp.zeros_like(carry_s)
        for at in reversed(range(nz)) if back else range(nz):

            @pl.when(at > mz if back else at < mz)
            def _():
                wait_all(tot_rcv.at[back, g, at], tr.at[back, g, at])
                factor = factors(at * ny, g)
                for y in range(1, ny):
                    factor = [a * b for a, b in zip(factor, factors(at * ny + y, g))]
                carry_s[...] = decayed(factor, carry_s[...]) + tot_rcv[back, g, at]

        carried = carry_s[...]
        for at in reversed(range(ny)) if back else range(ny):
            buf[g, at] = buf[g, at] + carried
            carried = decayed(factors(mz * ny + at, g), carried)

    def solve(g, between):
        state = [load_state(rcv2, g, i) for i in range(PAIR)]
        x, r, p, rr, keys, kts, big, gts = ([None] * PAIR for _ in range(8))
        for i in range(PAIR):
            h = g * PAIR + i
            qt = q_s[h].astype(F32).T
            gts[i] = ((g_s[h].astype(F32)).T * mask_lane).astype(BF16)
            gram, pair = split(state[i][0]), split(state[i][1])
            right = rhs_s[h] + sw_s[pl.ds(h, 1), :] * dot(
                jnp.concatenate(pair, axis=1), jnp.concatenate([gts[i], gts[i]], axis=0)
            )
            p[i] = r[i] = jnp.concatenate([qt, right], axis=1)
            rr[i] = jnp.sum(r[i] * r[i], axis=0, keepdims=True)
            keys[i] = (kv_s[h, 0, :, 0:DK], kv_s[h, 1, :, 0:DK])
            kts[i] = (kt_s[h, 0], kt_s[h, 1])
            big[i] = tuple(jnp.concatenate([a, b], axis=0) for a, b in zip(keys[i], gram))
        for it in range(ITERS):
            last = it == ITERS - 1
            for i in range(PAIR):
                h = g * PAIR + i
                table = jnp.concatenate([dt_s[h]] * 2, axis=1)
                sw = jnp.concatenate([sw_s[pl.ds(h, 1), :]] * 2, axis=1)
                if last:
                    both = dot(big[i][0], p[i].astype(BF16))
                    inner = dot(kts[i][0], (both[0:tokens] * table).astype(BF16))
                else:
                    both = dot3(big[i], split(p[i]))
                    inner = dot3(kts[i], split(both[0:tokens] * table))
                image = reg_ref[h] * p[i] + sw * both[tokens:] + inner
                size = rr[i] / (jnp.sum(p[i] * image, axis=0, keepdims=True) + TINY)
                x[i] = size * p[i] if it == 0 else x[i] + size * p[i]
                if not last:
                    r[i] = r[i] - size * image
                    following = jnp.sum(r[i] * r[i], axis=0, keepdims=True)
                    p[i] = r[i] + (following / (rr[i] + TINY)) * p[i]
                    rr[i] = following
            between[it]()
        grams, pairs, xns, ygs = [], [], [], []
        for i in range(PAIR):
            h = g * PAIR + i
            xt, yt = x[i][:, 0:tokens], x[i][:, tokens:]
            xn, yn = xt.T, yt.T
            qg_s[:, pl.ds(pl.multiple_of(h * DK, DK), DK)] = yn
            gn = (g_s[h].astype(F32) * mask_rows[:, 0:DK]).astype(BF16)
            y_high, y_low = split(yn)
            yg = (
                jnp.concatenate([y_high, gn], axis=1),
                jnp.concatenate([y_low, jnp.zeros_like(gn)], axis=1),
            )
            back = dot3(split(xt * sw_s[pl.ds(h, 1), :]), yg)
            grams.append(-(back[:, 0:DK] + back[:, 0:DK].T))
            pairs.append(back[:, DK:])
            xns.append(xn)
            ygs.append(yg)
        store_state(snd3, g, grams, pairs)
        across_y(snd3, rcv3, g, s3, r3)
        for i in range(PAIR):
            h = g * PAIR + i
            table = jnp.concatenate([dt_s[h]] * 2, axis=1)
            scores = dot3(keys[i], split(x[i])) * table
            sol, adj = scores[:, 0:tokens], scores[:, tokens:]
            from_x = dot3(split(vs_s[h] - adj), split(xns[i]))
            from_yg = dot3(split(sol), ygs[i])
            loc_s[h] = jnp.concatenate([from_x - from_yg[:, 0:DK], from_yg[:, DK:]], axis=1)

    def gradients(g):
        for i in range(PAIR):
            h = g * PAIR + i
            sym, pair_t = load_state(rcv4, g, i)
            pair = pair_t.T
            both = jnp.concatenate(
                [
                    jnp.concatenate([sym, pair_t], axis=1),
                    jnp.concatenate([pair, jnp.zeros_like(pair)], axis=1),
                ],
                axis=0,
            )
            carried = dot3((kv_s[h, 0], kv_s[h, 1]), split(both))
            decay = jnp.concatenate([ewc_s[h]] * 2, axis=1)
            grad = ((loc_s[h] + decay * carried) * mask_rows).astype(BF16)
            gr_s[g, 0:tokens, pl.ds(i * 2 * DK, 2 * DK)] = grad
            sib_snd[g, :, pl.ds(i * 2 * DK, 2 * DK)] = grad.astype(F32)

    def sib_copy(g):
        return pltpu.make_async_remote_copy(
            src_ref=sib_snd.at[g], dst_ref=sib_rcv.at[g], send_sem=sib_sem.at[0, g], recv_sem=sib_sem.at[1, g],
            device_id=(sib, ctx), device_id_type=MESH,
        )

    me = {"x": mx, "z": mz, "y": my}
    count = {"x": nx, "z": nz, "y": ny}
    whole = (wa, wb, wc)
    parts = [
        (order, rws, lns, bufs)
        for (order, rws, lns), bufs in zip(
            scatter_parts(rows), ((ra0, ra1, ra2, ra3), (rb0, rb1, rb2, rb3), (rc0, rc1, rc2, rc3))
        )
    ]

    def device(axis, at):
        place = dict(me)
        place[axis] = at
        return (place["x"] * 2 + mc, place["z"] * ny + place["y"])

    def chunk(n, part, g, at, side=None):
        order, rws, lns, bufs = parts[part]
        spot = (at,)
        if side is not None:
            half_count = count[order[1]] // 2
            spot = (at, pl.ds(side * half_count, half_count))
        if n == 0:
            return whole[part].at[(g,) + spot]
        return bufs[n].at[(g, 0) + spot]

    def send(src, dst, part, n, g, axis, to):
        pltpu.make_async_remote_copy(
            src_ref=src, dst_ref=dst, send_sem=rs_snd.at[part, n, g], recv_sem=rs_rcv.at[part, n, g],
            device_id=device(axis, to), device_id_type=MESH,
        ).start()

    def sides(axis):
        return lax.rem(me[axis] + 1, count[axis]), lax.rem(me[axis] + count[axis] - 1, count[axis])

    def scatter_far(g):
        for part, (order, rws, lns, bufs) in enumerate(parts):
            axis = order[0]
            if count[axis] == 4:
                for side, to in enumerate(sides(axis)):
                    far = lax.rem(me[axis] + 2, 4)
                    send(chunk(0, part, g, far, side), bufs[0].at[g, side], part, 0, g, axis, to)

    def scatter_near(g):
        for part, (order, rws, lns, bufs) in enumerate(parts):
            axis = order[0]
            if count[axis] == 4:
                wait_all(bufs[0].at[g], rs_rcv.at[part, 0, g])
                for side, to in enumerate(sides(axis)):
                    half_ref = chunk(0, part, g, to, side)
                    half_ref[...] = half_ref[...] + bufs[0][g, side]
                    send(chunk(0, part, g, to), bufs[1].at[g, side], part, 1, g, axis, to)
            else:
                scatter_direct(0, part, g)

    def scatter_direct(n, part, g):
        order, rws, lns, bufs = parts[part]
        axis = order[n]
        for o in range(1, count[axis]):
            to = lax.rem(me[axis] + o, count[axis])
            send(chunk(n, part, g, to), bufs[n + 1].at[g, o - 1], part, n + 1, g, axis, to)

    def scatter_start(n, g):
        for part in range(3):
            scatter_direct(n, part, g)

    def scatter_add(n, g):
        for part, (order, rws, lns, bufs) in enumerate(parts):
            summed = chunk(n, part, g, me[order[n]])[...]
            if count[order[n]] > 1:
                wait_all(bufs[n + 1].at[g], rs_rcv.at[part, n + 1, g])
                for o in range(bufs[n + 1].shape[1]):
                    summed = summed + bufs[n + 1][g, o]
            if n < 2:
                bufs[n + 1][g, 0] = summed
            else:
                first, second = (pl.ds((g * PAIR + i) * DK, DK) for i in range(PAIR))
                if part < 2:
                    kwg_ref[rws, first] = summed[:, 0:DK]
                    vwg_ref[rws, first] = summed[:, DK : 2 * DK]
                    kwg_ref[rws, second] = summed[:, 2 * DK :]
                else:
                    vwg_ref[rws, second] = summed

    def weight_part(g):
        sib_copy(g).wait_recv()
        gr_s[g, tokens:, :] = sib_rcv[g].astype(BF16)
        for k in range(nx):
            out = dot(xt_s[k * xb : (k + 1) * xb, :], gr_s[g])
            out = out.reshape(nz, ny, rows, PAIR * 2 * DK)
            for part, (order, rws, lns, bufs) in enumerate(parts):
                for z in range(nz):
                    for y in range(ny):
                        place = {"x": k, "z": z, "y": y}
                        whole[part][(g,) + tuple(place[a] for a in order)] = out[
                            z, y, rws.start : rws.start + rws.size, lns.start : lns.start + lns.size
                        ]
        scatter_far(g)

    def input_gradient():
        def columns(n, carry):
            span = pl.ds(pl.multiple_of(n * 256, 256), 256)
            total = None
            for h in range(heads):
                grad = gr_s[h // PAIR, 0:tokens, (h % PAIR) * 2 * DK : (h % PAIR + 1) * 2 * DK]
                term = lax.dot_general(
                    grad, w_s[h, span, :], (((1,), (1,)), ((), ())), preferred_element_type=F32
                )
                total = term if total is None else total + term
            ig_s[:, span] = total.astype(BF16)
            return carry

        lax.fori_loop(0, width // 256, columns, 0)

    def forward_y(g):
        wait_others(rcv1, g, r1)
        prefix_y(rcv1, g, 0)

    def forward_z(g):
        prefix_z(rcv1, g, 0)
        across_y(rcv1, rcv2, g, s2, r2)

    def backward_y(g):
        wait_others(rcv3, g, r3)
        prefix_y(rcv3, g, 1)

    def backward_z(g):
        prefix_z(rcv3, g, 1)
        across_y(rcv3, rcv4, g, s4, r4)

    def backward_grads(g):
        wait_others(rcv4, g, r4)
        gradients(g)
        sib_copy(g).start()

    def reduce_two(g):
        scatter_add(0, g)
        scatter_start(1, g)

    def reduce_three(g):
        scatter_add(1, g)
        scatter_start(2, g)

    def reduce_last(g):
        scatter_add(2, g)

    def send_state(g):
        across_y(snd1, rcv1, g, s1, r1)

    wait_all(x_s, ld_sem.at[0])
    project(0)
    pl.semaphore_wait(barrier, nctx - 1 + 1 + nx - 1)
    send_state(0)
    for o in range(1, nctx):
        to = lax.rem(ctx + o, nctx)
        pltpu.make_async_remote_copy(
            src_ref=fac_snd, dst_ref=fac_rcv.at[ctx], send_sem=fac_sem.at[0], recv_sem=fac_sem.at[1],
            device_id=(dp, to), device_id_type=MESH,
        ).start()
    fac_rcv[ctx] = fac_snd[...]
    project(1)
    send_state(1)
    wait_all(g_s, ld_sem.at[1])
    wait_all(q_s, ld_sem.at[2])
    tables(0)
    tables(1)
    wait_all(fac_rcv.at[pl.ds(0, nctx - 1)], fac_sem.at[1])
    forward_y(0)
    project(2)
    forward_y(1)
    forward_z(0)
    send_state(2)
    forward_z(1)
    for k in range(nx):
        theirs = pl.ds(pl.multiple_of(k * 2 * xb + (1 - mc) * xb, xb), xb)
        xs_snd[:, k * xb : (k + 1) * xb] = x_s[:, theirs].astype(F32)
    x_copy = pltpu.make_async_remote_copy(
        src_ref=xs_snd, dst_ref=xs_rcv, send_sem=x_sem.at[0], recv_sem=x_sem.at[1],
        device_id=(sib, ctx), device_id_type=MESH,
    )
    x_copy.start()
    project(3)
    send_state(3)
    tables(2)
    tables(3)
    for k in range(nx):
        mine = pl.ds(pl.multiple_of(k * 2 * xb + mc * xb, xb), xb)
        xt_s[k * xb : (k + 1) * xb, 0:tokens] = x_s[:, mine].astype(F32).T.astype(BF16)

    def during(s, first, fn, count=groups):
        @pl.when(jnp.logical_and(s >= first, s < first + count))
        def _():
            fn(s - first)

    def with_solve(s, carry):
        def zero():
            during(s, 3, weight_part)
            pl.when(s == 0)(lambda: forward_y(2))

        def one():
            pl.when(s == 0)(lambda: forward_y(3))
            during(s, 2, backward_z)

        def two():
            pl.when(s == 0)(lambda: forward_z(2))

        def three():
            pl.when(s == 0)(lambda: forward_z(3))
            during(s, 1, backward_y)
            during(s, 3, scatter_near)

        wait_others(rcv2, s, r2)
        solve(s, (zero, one, two, three))
        during(s, 2, backward_grads)

        @pl.when(s == 0)
        def _():
            x_copy.wait_recv()
            for k in range(nx):
                xt_s[k * xb : (k + 1) * xb, tokens:] = xs_rcv[:, k * xb : (k + 1) * xb].T.astype(BF16)

        return carry

    lax.fori_loop(0, groups, with_solve, 0)
    qg_copy = pltpu.make_async_copy(qg_s, qg_ref.at[0], out_sem.at[0])
    qg_copy.start()
    backward_z(2)
    weight_part(1)
    backward_y(3)
    backward_grads(2)
    scatter_near(1)
    backward_z(3)
    weight_part(2)
    reduce_two(0)
    backward_grads(3)
    scatter_near(2)
    weight_part(3)
    reduce_two(1)
    reduce_three(0)
    input_gradient()
    ig_copy = pltpu.make_async_copy(ig_s, ig_ref.at[0], out_sem.at[1])
    ig_copy.start()
    scatter_near(3)
    reduce_two(2)
    reduce_three(1)
    reduce_last(0)
    reduce_two(3)
    reduce_three(2)
    reduce_last(1)
    reduce_three(3)
    reduce_last(2)
    reduce_last(3)

    qg_copy.wait()
    ig_copy.wait()
    sent = pltpu.make_async_copy(
        fac_rcv.at[pl.ds(0, nctx - 1)], fac_rcv.at[pl.ds(0, nctx - 1)], fac_sem.at[0]
    )
    sent.wait()
    x_copy.wait_send()

    def drain(g, carry):
        wait_sent(snd1, g, s1)
        wait_sent(rcv1, g, s2)
        wait_sent(snd3, g, s3)
        wait_sent(rcv3, g, s4)
        sib_copy(g).wait_send()
        for part, (order, rws, lns, bufs) in enumerate(parts):
            for n in range(4):
                if count[order[max(n - 1, 0)]] > 1 and (n > 0 or count[order[0]] == 4):
                    wait_all(bufs[n].at[g], rs_snd.at[part, n, g])
        for back in range(2):
            for o in range(1, nz):
                to = lax.rem(mz + o, nz)

                @pl.when(to < mz if back else to > mz)
                def _():
                    total_copy(back, g, to).wait_send()

        return carry

    lax.fori_loop(0, groups, drain, 0)


def copy_kernel(a, b, c, d, a_out, b_out, c_out, d_out):
    for src, dst in ((a, a_out), (b, b_out), (c, c_out), (d, d_out)):
        dst[...] = src[...]


def copied(arrays):
    steps = 2
    specs = [
        pl.BlockSpec((1, a.shape[1] // steps, a.shape[2]), lambda i: (0, i, 0))
        if len(a.shape) == 3
        else pl.BlockSpec((a.shape[0] // steps, a.shape[1]), lambda i: (i, 0))
        for a in arrays
    ]
    return pl.pallas_call(
        copy_kernel,
        out_shape=tuple(jax.ShapeDtypeStruct(a.shape, a.dtype) for a in arrays),
        grid=(steps,),
        in_specs=specs,
        out_specs=tuple(specs),
        compiler_params=pltpu.CompilerParams(vmem_limit_bytes=62 << 20),
        name="results",
    )(*arrays)


def scatter_parts(rows):
    return (
        ("xyz", pl.ds(0, rows // 2), pl.ds(0, 3 * DK)),
        ("zxy", pl.ds(rows // 2, rows // 2), pl.ds(0, 3 * DK)),
        ("yzx", pl.ds(0, rows), pl.ds(3 * DK, DK)),
    )


def solution(mesh):
    nx = mesh.shape["dp"] // 2
    nctx = mesh.shape["ctx"]
    ny = min(nctx, 4)
    nz = nctx // ny

    def body(layer_input, queries, gates, regularizer, key_weight, value_weight, out_cotangent, lengths):
        tokens, width = layer_input.shape[1:]
        heads = gates.shape[2]
        groups = heads // PAIR
        rows = width // (2 * nx * nctx)
        tiles = PAIR * 24 // ny + 1
        wide = PAIR * 2 * DK
        state = lambda: pltpu.VMEM((groups, ny, tiles, 8, DK), F32)
        dma = lambda *shape: pltpu.SemaphoreType.DMA(shape)
        scratch = [
            pltpu.VMEM((tokens, width), BF16),
            pltpu.VMEM((heads, width, 2 * DK), BF16),
            pltpu.VMEM((heads, tokens, DK), BF16),
            pltpu.VMEM((heads, tokens, DK), BF16),
            pltpu.VMEM((tokens, width), BF16),
            pltpu.VMEM((tokens, heads * DK), F32),
            pltpu.VMEM((heads, tokens), F32),
            pltpu.VMEM((heads, tokens), F32),
            pltpu.VMEM((heads, tokens), F32),
            pltpu.VMEM((heads, tokens), F32),
            pltpu.VMEM((heads, DK), F32),
            pltpu.VMEM((nctx, heads, DK), F32),
            pltpu.VMEM((heads, 2, tokens, 2 * DK), BF16),
            pltpu.VMEM((heads, 2, DK, tokens), BF16),
            pltpu.VMEM((heads, tokens, tokens), F32),
            pltpu.VMEM((heads, tokens, tokens), F32),
            pltpu.VMEM((heads, DK, tokens), F32),
            pltpu.VMEM((heads, tokens, DK), F32),
            pltpu.VMEM((heads, tokens, 2 * DK), F32),
            state(), state(), state(), state(), state(), state(),
            pltpu.VMEM((2, groups, tiles, 8, DK), F32),
            pltpu.VMEM((2, groups, nz, tiles, 8, DK), F32),
            pltpu.VMEM((tiles, 8, DK), F32),
            pltpu.VMEM((tokens, width // 2), F32),
            pltpu.VMEM((tokens, width // 2), F32),
            pltpu.VMEM((width // 2, 2 * tokens), BF16),
            pltpu.VMEM((groups, 2 * tokens, wide), BF16),
            pltpu.VMEM((groups, tokens, wide), F32),
            pltpu.VMEM((groups, tokens, wide), F32),
        ]
        count = {"x": nx, "z": nz, "y": ny}
        for order, rws, lns in scatter_parts(rows):
            a, b, c = (count[axis] for axis in order)
            scratch.append(pltpu.VMEM((groups, a, b, c, rws.size, lns.size), F32))
            scratch.append(pltpu.VMEM((groups, 2, max(b // 2, 1), c, rws.size, lns.size), F32))
            for n in range(3):
                slots = 2 if n == 0 and count[order[0]] == 4 else max(count[order[n]] - 1, 1)
                left = tuple(count[a] for a in order[n + 1 :])
                scratch.append(pltpu.VMEM((groups, slots) + left + (rws.size, lns.size), F32))
        scratch += [dma(2), dma(3), dma(heads), dma(2), dma(2), dma(2, groups)]
        scratch += [dma(groups)] * 8 + [dma(2, groups, nz)] * 2 + [dma(3, 4, groups)] * 2
        any_space = pl.BlockSpec(memory_space=pl.ANY)
        vmem = pl.BlockSpec(memory_space=pltpu.VMEM)
        smem = pl.BlockSpec(memory_space=pltpu.SMEM)
        results = pl.pallas_call(
            functools.partial(mesa_kernel, (nx, nz, ny, heads, tokens, width)),
            out_shape=(
                jax.ShapeDtypeStruct((1, tokens, width), BF16),
                jax.ShapeDtypeStruct((1, tokens, heads * DK), F32),
                jax.ShapeDtypeStruct((rows, heads * DK), F32),
                jax.ShapeDtypeStruct((rows, heads * DK), F32),
            ),
            in_specs=[any_space, any_space, vmem, smem, any_space, any_space, any_space, smem],
            out_specs=(any_space, any_space, vmem, vmem),
            scratch_shapes=scratch,
            compiler_params=pltpu.CompilerParams(
                collective_id=0, has_side_effects=True, vmem_limit_bytes=63 << 20
            ),
            name="mesa_backward",
        )(layer_input, queries, jnp.swapaxes(gates, 1, 2), regularizer, key_weight, value_weight, out_cotangent, lengths)
        return copied(results)

    in_specs = (
        P("dp", "ctx", None),
        P("dp", "ctx", None),
        P("dp", "ctx", None),
        P(),
        P(),
        P(),
        P("dp", "ctx", None),
        P("dp", "ctx"),
    )
    out_specs = (
        P("dp", "ctx", None),
        P("dp", "ctx", None),
        P(("dp", "ctx"), None),
        P(("dp", "ctx"), None),
    )
    return jax.shard_map(body, mesh=mesh, in_specs=in_specs, out_specs=out_specs, check_vma=False)
```

```python
import functools

import jax
import jax.numpy as jnp
from jax import lax
from jax.experimental import pallas as pl
from jax.experimental.pallas import tpu as pltpu
from jax.sharding import PartitionSpec as P

ITERS = 4
TINY = 1e-06
DK = 128
PAIR = 2
F32 = jnp.float32
BF16 = jnp.bfloat16
MESH = pl.DeviceIdType.MESH


def split(a):
    high = a.astype(BF16)
    return high, (a - high.astype(F32)).astype(BF16)


def dot(a, b):
    return jnp.dot(a, b, preferred_element_type=F32)


def left3(parts):
    high, low = parts
    return jnp.concatenate([high, low, high], axis=1)


def right3(parts):
    high, low = parts
    return jnp.concatenate([high, high, low], axis=0)


def dot3(a, b):
    return dot(left3(a), right3(b))


def pack(sym):
    half = DK // 2
    row = lax.broadcasted_iota(jnp.int32, (half, DK), 0)
    lane = lax.broadcasted_iota(jnp.int32, (half, DK), 1)
    low = pltpu.roll(sym[half:], half, 1)
    diag = jnp.sum(jnp.where(lane == row, low, 0.0), axis=0, keepdims=True)
    return jnp.where(lane < row, low, sym[0:half]), diag


def unpack(packed, diag):
    half = DK // 2
    row = lax.broadcasted_iota(jnp.int32, (half, DK), 0)
    lane = lax.broadcasted_iota(jnp.int32, (half, DK), 1)
    diag = pltpu.roll(jnp.broadcast_to(diag, (half, DK)), half, 1)
    upper = jnp.where(lane > row, packed, 0.0)
    lower = pltpu.roll(jnp.where(lane < row, packed, 0.0), half, 1)
    off = jnp.concatenate([upper, lower], axis=0)
    on = jnp.concatenate(
        [jnp.where(lane == row, packed, 0.0), jnp.where(lane == row + half, diag, 0.0)], axis=0
    )
    return off + off.T + on


def mesa_kernel(
    sizes,
    x_ref, q_ref, gates_ref, reg_ref, wk_ref, wv_ref, g_ref, len_ref,
    ig_ref, qg_ref, kwg_ref, vwg_ref,
    x_s, w_s, q_s, g_s, ig_s, qg_s, run_s, tot_s, sw_s, ew_s, fac_snd, fac_rcv,
    kv_s, kt_s, dt_s, vs_s, rhs_s, ewc_s, loc_s,
    snd1, rcv1, rcv2, snd3, rcv3, rcv4, tot_snd, tot_rcv, carry_s,
    xs_snd, xs_rcv, xt_s, gr_s, sib_snd, sib_rcv,
    wa, ra0, ra1, ra2, ra3, wb, rb0, rb1, rb2, rb3, wc, rc0, rc1, rc2, rc3,
    out_sem, ld_sem, w_sem, fac_sem, x_sem, sib_sem, s1, r1, s2, r2, s3, r3, s4, r4, ts, tr, rs_snd, rs_rcv,
):
    nx, nz, ny, heads, tokens, width = sizes
    nctx = nz * ny
    groups = heads // PAIR
    per = 24 // ny
    gram_rows, pair_rows = DK // 2 // ny, DK // ny
    xb = width // (2 * nx)
    rows = xb // nctx
    half = rows // 2
    dp, ctx = lax.axis_index("dp"), lax.axis_index("ctx")
    mx, mc = lax.div(dp, 2), lax.rem(dp, 2)
    mz, my = lax.div(ctx, ny), lax.rem(ctx, ny)
    sib = mx * 2 + (1 - mc)

    barrier = pltpu.get_barrier_semaphore()
    for o in range(1, nctx):
        pl.semaphore_signal(barrier, inc=1, device_id=(dp, lax.rem(ctx + o, nctx)), device_id_type=MESH)
    pl.semaphore_signal(barrier, inc=1, device_id=(sib, ctx), device_id_type=MESH)
    for o in range(1, nx):
        pl.semaphore_signal(
            barrier, inc=1, device_id=(lax.rem(mx + o, nx) * 2 + mc, ctx), device_id_type=MESH
        )

    pltpu.make_async_copy(x_ref.at[0], x_s, ld_sem.at[0]).start()
    def load_weights(h):
        cols = pl.ds(h * DK, DK)
        pltpu.make_async_copy(wk_ref.at[:, cols], w_s.at[h, :, pl.ds(0, DK)], w_sem.at[h]).start()
        pltpu.make_async_copy(wv_ref.at[:, cols], w_s.at[h, :, pl.ds(DK, DK)], w_sem.at[h]).start()

    for h in range(heads):
        load_weights(h)
    for h in range(heads):
        cols = pl.ds(h * DK, DK)
        pltpu.make_async_copy(g_ref.at[0, :, cols], g_s.at[h], ld_sem.at[1]).start()
        pltpu.make_async_copy(q_ref.at[0, :, cols], q_s.at[h], ld_sem.at[2]).start()

    length = len_ref[0, 0]
    run = jnp.log(gates_ref[0])
    lane = lax.broadcasted_iota(jnp.int32, (heads, tokens), 1)
    step = 1
    while step < tokens:
        run = run + jnp.where(lane >= step, pltpu.roll(run, step, 1), 0.0)
        step *= 2
    total = jnp.broadcast_to(run[:, tokens - 1 : tokens], (heads, tokens))
    run_s[...] = run
    tot_s[...] = total
    sw_s[...] = jnp.exp(run)
    ew_s[...] = jnp.exp(total - run)
    fac_snd[...] = jnp.exp(total[:, 0:DK])

    mask_rows = (lax.broadcasted_iota(jnp.int32, (tokens, 2 * DK), 0) < length).astype(F32)
    mask_lane = (lax.broadcasted_iota(jnp.int32, (1, tokens), 1) < length).astype(F32)

    def across_y(src, dst, g, send, recv):
        for o in sorted(range(1, ny), key=lambda o: -min(o, ny - o)):
            to = lax.rem(my + o, ny)
            pltpu.make_async_remote_copy(
                src_ref=src.at[g, to], dst_ref=dst.at[g, my], send_sem=send.at[g], recv_sem=recv.at[g],
                device_id=(dp, mz * ny + to), device_id_type=MESH,
            ).start()
        dst[g, my] = src[g, my]

    def wait_all(buf, sem):
        pltpu.make_async_copy(buf, buf, sem).wait()

    def wait_others(buf, g, sem):
        wait_all(buf.at[g, pl.ds(0, ny - 1)], sem.at[g])

    def wait_sent(buf, g, sem):
        part = buf.at[g, pl.ds(0, ny - 1)]
        pltpu.make_async_copy(part, part, sem.at[g]).wait()

    def store_state(buf, g, grams, pairs):
        head = lax.broadcasted_iota(jnp.int32, (heads, DK), 0)
        diags = jnp.zeros((heads, DK), F32)
        for i in range(PAIR):
            packed, diag = pack(grams[i])
            diags = jnp.where(head == g * PAIR + i, diag, diags)
            for to in range(ny):
                buf[g, to, i * per : i * per + per // 3] = packed[
                    to * gram_rows : (to + 1) * gram_rows
                ].reshape(per // 3, 8, DK)
                buf[g, to, i * per + per // 3 : (i + 1) * per] = pairs[i][
                    to * pair_rows : (to + 1) * pair_rows
                ].reshape(2 * per // 3, 8, DK)
        for to in range(ny):
            buf[g, to, PAIR * per] = diags

    def load_state(buf, g, i):
        head = lax.broadcasted_iota(jnp.int32, (heads, DK), 0)
        diag = jnp.sum(jnp.where(head == g * PAIR + i, buf[g, 0, PAIR * per], 0.0), axis=0, keepdims=True)
        packed = jnp.concatenate(
            [buf[g, at, i * per : i * per + per // 3].reshape(gram_rows, DK) for at in range(ny)], axis=0
        )
        pair = jnp.concatenate(
            [buf[g, at, i * per + per // 3 : (i + 1) * per].reshape(pair_rows, DK) for at in range(ny)],
            axis=0,
        )
        return unpack(packed, diag), pair

    def factors(c, g):
        return [fac_rcv[c, pl.ds(g * PAIR + i, 1), :] for i in range(PAIR)] + [fac_rcv[c]]

    def decayed(factor, tiles):
        scaled = [tiles[i * per : (i + 1) * per] * factor[i] for i in range(PAIR)]
        return jnp.concatenate(scaled + [tiles[PAIR * per :] * factor[PAIR]], axis=0)

    def project(g):
        grams, pairs = [], []
        for i in range(PAIR):
            h = g * PAIR + i
            wait_all(w_s.at[h], w_sem.at[h])
            kv = dot(x_s[...], w_s[h]) * mask_rows
            parts = split(kv)
            kv_s[h, 0], kv_s[h, 1] = parts
            kt = kv[:, 0:DK].T
            kt_s[h, 0], kt_s[h, 1] = split(kt)
            state = dot3(split(kt * ew_s[pl.ds(h, 1), :]), parts)
            grams.append(state[:, 0:DK])
            pairs.append(state[:, DK:])
        store_state(snd1, g, grams, pairs)

    def tables(g):
        for i in range(PAIR):
            h = g * PAIR + i
            run_row = run_s[pl.ds(h, 1), :]
            run_col = jnp.broadcast_to(run_row, (DK, tokens)).T
            ewc_s[h] = jnp.exp(tot_s[pl.ds(h, 1), :][:, 0:DK] - run_col)
            gap = run_row - jnp.concatenate([run_col] * (tokens // DK), axis=1)
            later = lax.broadcasted_iota(jnp.int32, (tokens, tokens), 1) >= lax.broadcasted_iota(
                jnp.int32, (tokens, tokens), 0
            )
            table = jnp.exp(jnp.where(later, gap, -1e30))
            dt_s[h] = table
            gt = ((g_s[h].astype(F32)).T * mask_lane).astype(BF16)
            v_both = jnp.concatenate([kv_s[h, 0, :, DK:], kv_s[h, 1, :, DK:]], axis=1)
            scores = dot(v_both, jnp.concatenate([gt, gt], axis=0)) * table
            vs_s[h] = scores
            rhs_s[h] = dot3((kt_s[h, 0], kt_s[h, 1]), split(scores))

    def prefix_y(buf, g, back):
        held = None
        for at in reversed(range(ny)) if back else range(ny):
            mine = buf[g, at]
            if held is None:
                buf[g, at] = jnp.zeros_like(mine)
                held = mine
            else:
                buf[g, at] = held
                held = decayed(factors(mz * ny + at, g), held) + mine
        tot_snd[back, g] = held
        for o in range(1, nz):
            to = lax.rem(mz + o, nz)

            @pl.when(to < mz if back else to > mz)
            def _():
                total_copy(back, g, to).start()

    def total_copy(back, g, to):
        return pltpu.make_async_remote_copy(
            src_ref=tot_snd.at[back, g], dst_ref=tot_rcv.at[back, g, mz],
            send_sem=ts.at[back, g, to], recv_sem=tr.at[back, g, mz],
            device_id=(dp, to * ny + my), device_id_type=MESH,
        )

    def prefix_z(buf, g, back):
        carry_s[...] = jnp.zeros_like(carry_s)
        for at in reversed(range(nz)) if back else range(nz):

            @pl.when(at > mz if back else at < mz)
            def _():
                wait_all(tot_rcv.at[back, g, at], tr.at[back, g, at])
                factor = factors(at * ny, g)
                for y in range(1, ny):
                    factor = [a * b for a, b in zip(factor, factors(at * ny + y, g))]
                carry_s[...] = decayed(factor, carry_s[...]) + tot_rcv[back, g, at]

        carried = carry_s[...]
        for at in reversed(range(ny)) if back else range(ny):
            buf[g, at] = buf[g, at] + carried
            carried = decayed(factors(mz * ny + at, g), carried)

    def solve(g, between):
        state = [load_state(rcv2, g, i) for i in range(PAIR)]
        x, r, p, rr, keys, kts, big, gts = ([None] * PAIR for _ in range(8))
        for i in range(PAIR):
            h = g * PAIR + i
            qt = q_s[h].astype(F32).T
            gts[i] = ((g_s[h].astype(F32)).T * mask_lane).astype(BF16)
            gram, pair = split(state[i][0]), split(state[i][1])
            right = rhs_s[h] + sw_s[pl.ds(h, 1), :] * dot(
                jnp.concatenate(pair, axis=1), jnp.concatenate([gts[i], gts[i]], axis=0)
            )
            p[i] = r[i] = jnp.concatenate([qt, right], axis=1)
            rr[i] = jnp.sum(r[i] * r[i], axis=0, keepdims=True)
            keys[i] = (kv_s[h, 0, :, 0:DK], kv_s[h, 1, :, 0:DK])
            kts[i] = (kt_s[h, 0], kt_s[h, 1])
            big[i] = tuple(jnp.concatenate([a, b], axis=0) for a, b in zip(keys[i], gram))
        for it in range(ITERS):
            last = it == ITERS - 1
            for i in range(PAIR):
                h = g * PAIR + i
                table = jnp.concatenate([dt_s[h]] * 2, axis=1)
                sw = jnp.concatenate([sw_s[pl.ds(h, 1), :]] * 2, axis=1)
                if last:
                    both = dot(big[i][0], p[i].astype(BF16))
                    inner = dot(kts[i][0], (both[0:tokens] * table).astype(BF16))
                else:
                    both = dot3(big[i], split(p[i]))
                    inner = dot3(kts[i], split(both[0:tokens] * table))
                image = reg_ref[h] * p[i] + sw * both[tokens:] + inner
                size = rr[i] / (jnp.sum(p[i] * image, axis=0, keepdims=True) + TINY)
                x[i] = size * p[i] if it == 0 else x[i] + size * p[i]
                if not last:
                    r[i] = r[i] - size * image
                    following = jnp.sum(r[i] * r[i], axis=0, keepdims=True)
                    p[i] = r[i] + (following / (rr[i] + TINY)) * p[i]
                    rr[i] = following
            between[it]()
        grams, pairs, xns, ygs = [], [], [], []
        for i in range(PAIR):
            h = g * PAIR + i
            xt, yt = x[i][:, 0:tokens], x[i][:, tokens:]
            xn, yn = xt.T, yt.T
            qg_s[:, pl.ds(pl.multiple_of(h * DK, DK), DK)] = yn
            gn = (g_s[h].astype(F32) * mask_rows[:, 0:DK]).astype(BF16)
            y_high, y_low = split(yn)
            yg = (
                jnp.concatenate([y_high, gn], axis=1),
                jnp.concatenate([y_low, jnp.zeros_like(gn)], axis=1),
            )
            back = dot3(split(xt * sw_s[pl.ds(h, 1), :]), yg)
            grams.append(-(back[:, 0:DK] + back[:, 0:DK].T))
            pairs.append(back[:, DK:])
            xns.append(xn)
            ygs.append(yg)
        store_state(snd3, g, grams, pairs)
        across_y(snd3, rcv3, g, s3, r3)
        for i in range(PAIR):
            h = g * PAIR + i
            table = jnp.concatenate([dt_s[h]] * 2, axis=1)
            scores = dot3(keys[i], split(x[i])) * table
            sol, adj = scores[:, 0:tokens], scores[:, tokens:]
            from_x = dot3(split(vs_s[h] - adj), split(xns[i]))
            from_yg = dot3(split(sol), ygs[i])
            loc_s[h] = jnp.concatenate([from_x - from_yg[:, 0:DK], from_yg[:, DK:]], axis=1)

    def gradients(g):
        for i in range(PAIR):
            h = g * PAIR + i
            sym, pair_t = load_state(rcv4, g, i)
            pair = pair_t.T
            both = jnp.concatenate(
                [
                    jnp.concatenate([sym, pair_t], axis=1),
                    jnp.concatenate([pair, jnp.zeros_like(pair)], axis=1),
                ],
                axis=0,
            )
            carried = dot3((kv_s[h, 0], kv_s[h, 1]), split(both))
            decay = jnp.concatenate([ewc_s[h]] * 2, axis=1)
            grad = ((loc_s[h] + decay * carried) * mask_rows).astype(BF16)
            gr_s[g, 0:tokens, pl.ds(i * 2 * DK, 2 * DK)] = grad
            sib_snd[g, :, pl.ds(i * 2 * DK, 2 * DK)] = grad.astype(F32)

    def sib_copy(g):
        return pltpu.make_async_remote_copy(
            src_ref=sib_snd.at[g], dst_ref=sib_rcv.at[g], send_sem=sib_sem.at[0, g], recv_sem=sib_sem.at[1, g],
            device_id=(sib, ctx), device_id_type=MESH,
        )

    me = {"x": mx, "z": mz, "y": my}
    count = {"x": nx, "z": nz, "y": ny}
    whole = (wa, wb, wc)
    parts = [
        (order, rws, lns, bufs)
        for (order, rws, lns), bufs in zip(
            scatter_parts(rows), ((ra0, ra1, ra2, ra3), (rb0, rb1, rb2, rb3), (rc0, rc1, rc2, rc3))
        )
    ]

    def device(axis, at):
        place = dict(me)
        place[axis] = at
        return (place["x"] * 2 + mc, place["z"] * ny + place["y"])

    def chunk(n, part, g, at, side=None):
        order, rws, lns, bufs = parts[part]
        spot = (at,)
        if side is not None:
            half_count = count[order[1]] // 2
            spot = (at, pl.ds(side * half_count, half_count))
        if n == 0:
            return whole[part].at[(g,) + spot]
        return bufs[n].at[(g, 0) + spot]

    def send(src, dst, part, n, g, axis, to):
        pltpu.make_async_remote_copy(
            src_ref=src, dst_ref=dst, send_sem=rs_snd.at[part, n, g], recv_sem=rs_rcv.at[part, n, g],
            device_id=device(axis, to), device_id_type=MESH,
        ).start()

    def sides(axis):
        return lax.rem(me[axis] + 1, count[axis]), lax.rem(me[axis] + count[axis] - 1, count[axis])

    def scatter_far(g):
        for part, (order, rws, lns, bufs) in enumerate(parts):
            axis = order[0]
            if count[axis] == 4:
                for side, to in enumerate(sides(axis)):
                    far = lax.rem(me[axis] + 2, 4)
                    send(chunk(0, part, g, far, side), bufs[0].at[g, side], part, 0, g, axis, to)

    def scatter_near(g):
        for part, (order, rws, lns, bufs) in enumerate(parts):
            axis = order[0]
            if count[axis] == 4:
                wait_all(bufs[0].at[g], rs_rcv.at[part, 0, g])
                for side, to in enumerate(sides(axis)):
                    half_ref = chunk(0, part, g, to, side)
                    half_ref[...] = half_ref[...] + bufs[0][g, side]
                    send(chunk(0, part, g, to), bufs[1].at[g, side], part, 1, g, axis, to)
            else:
                scatter_direct(0, part, g)

    def scatter_direct(n, part, g):
        order, rws, lns, bufs = parts[part]
        axis = order[n]
        for o in range(1, count[axis]):
            to = lax.rem(me[axis] + o, count[axis])
            send(chunk(n, part, g, to), bufs[n + 1].at[g, o - 1], part, n + 1, g, axis, to)

    def scatter_start(n, g):
        for part in range(3):
            scatter_direct(n, part, g)

    def scatter_add(n, g):
        for part, (order, rws, lns, bufs) in enumerate(parts):
            summed = chunk(n, part, g, me[order[n]])[...]
            if count[order[n]] > 1:
                wait_all(bufs[n + 1].at[g], rs_rcv.at[part, n + 1, g])
                for o in range(bufs[n + 1].shape[1]):
                    summed = summed + bufs[n + 1][g, o]
            if n < 2:
                bufs[n + 1][g, 0] = summed
            else:
                first, second = (pl.ds((g * PAIR + i) * DK, DK) for i in range(PAIR))
                if part < 2:
                    kwg_ref[rws, first] = summed[:, 0:DK]
                    vwg_ref[rws, first] = summed[:, DK : 2 * DK]
                    kwg_ref[rws, second] = summed[:, 2 * DK :]
                else:
                    vwg_ref[rws, second] = summed

    def weight_part(g):
        sib_copy(g).wait_recv()
        gr_s[g, tokens:, :] = sib_rcv[g].astype(BF16)
        for k in range(nx):
            out = dot(xt_s[k * xb : (k + 1) * xb, :], gr_s[g])
            out = out.reshape(nz, ny, rows, PAIR * 2 * DK)
            for part, (order, rws, lns, bufs) in enumerate(parts):
                for z in range(nz):
                    for y in range(ny):
                        place = {"x": k, "z": z, "y": y}
                        whole[part][(g,) + tuple(place[a] for a in order)] = out[
                            z, y, rws.start : rws.start + rws.size, lns.start : lns.start + lns.size
                        ]
        scatter_far(g)

    def input_gradient():
        def columns(n, carry):
            span = pl.ds(pl.multiple_of(n * 256, 256), 256)
            total = None
            for h in range(heads):
                grad = gr_s[h // PAIR, 0:tokens, (h % PAIR) * 2 * DK : (h % PAIR + 1) * 2 * DK]
                term = lax.dot_general(
                    grad, w_s[h, span, :], (((1,), (1,)), ((), ())), preferred_element_type=F32
                )
                total = term if total is None else total + term
            ig_s[:, span] = total.astype(BF16)
            return carry

        lax.fori_loop(0, width // 256, columns, 0)

    def forward_y(g):
        wait_others(rcv1, g, r1)
        prefix_y(rcv1, g, 0)

    def forward_z(g):
        prefix_z(rcv1, g, 0)
        across_y(rcv1, rcv2, g, s2, r2)

    def backward_y(g):
        wait_others(rcv3, g, r3)
        prefix_y(rcv3, g, 1)

    def backward_z(g):
        prefix_z(rcv3, g, 1)
        across_y(rcv3, rcv4, g, s4, r4)

    def backward_grads(g):
        wait_others(rcv4, g, r4)
        gradients(g)
        sib_copy(g).start()

    def reduce_two(g):
        scatter_add(0, g)
        scatter_start(1, g)

    def reduce_three(g):
        scatter_add(1, g)
        scatter_start(2, g)

    def reduce_last(g):
        scatter_add(2, g)

    def send_state(g):
        across_y(snd1, rcv1, g, s1, r1)

    wait_all(x_s, ld_sem.at[0])
    project(0)
    pl.semaphore_wait(barrier, nctx - 1 + 1 + nx - 1)
    send_state(0)
    for o in range(1, nctx):
        to = lax.rem(ctx + o, nctx)
        pltpu.make_async_remote_copy(
            src_ref=fac_snd, dst_ref=fac_rcv.at[ctx], send_sem=fac_sem.at[0], recv_sem=fac_sem.at[1],
            device_id=(dp, to), device_id_type=MESH,
        ).start()
    fac_rcv[ctx] = fac_snd[...]
    project(1)
    send_state(1)
    wait_all(g_s, ld_sem.at[1])
    wait_all(q_s, ld_sem.at[2])
    tables(0)
    tables(1)
    wait_all(fac_rcv.at[pl.ds(0, nctx - 1)], fac_sem.at[1])
    forward_y(0)
    project(2)
    forward_y(1)
    forward_z(0)
    send_state(2)
    forward_z(1)
    for k in range(nx):
        theirs = pl.ds(pl.multiple_of(k * 2 * xb + (1 - mc) * xb, xb), xb)
        xs_snd[:, k * xb : (k + 1) * xb] = x_s[:, theirs].astype(F32)
    x_copy = pltpu.make_async_remote_copy(
        src_ref=xs_snd, dst_ref=xs_rcv, send_sem=x_sem.at[0], recv_sem=x_sem.at[1],
        device_id=(sib, ctx), device_id_type=MESH,
    )
    x_copy.start()
    project(3)
    send_state(3)
    tables(2)
    tables(3)
    for k in range(nx):
        mine = pl.ds(pl.multiple_of(k * 2 * xb + mc * xb, xb), xb)
        xt_s[k * xb : (k + 1) * xb, 0:tokens] = x_s[:, mine].astype(F32).T.astype(BF16)

    def during(s, first, fn, count=groups):
        @pl.when(jnp.logical_and(s >= first, s < first + count))
        def _():
            fn(s - first)

    def with_solve(s, carry):
        def zero():
            during(s, 2, backward_z)
            during(s, 3, weight_part)
            pl.when(s == 0)(lambda: forward_y(2))

        def one():
            pl.when(s == 0)(lambda: forward_y(3))

        def two():
            pl.when(s == 0)(lambda: forward_z(2))
            during(s, 1, backward_y)

        def three():
            pl.when(s == 0)(lambda: forward_z(3))
            during(s, 3, scatter_near)

        wait_others(rcv2, s, r2)
        solve(s, (zero, one, two, three))
        during(s, 2, backward_grads)

        @pl.when(s == 0)
        def _():
            x_copy.wait_recv()
            for k in range(nx):
                xt_s[k * xb : (k + 1) * xb, tokens:] = xs_rcv[:, k * xb : (k + 1) * xb].T.astype(BF16)

        return carry

    lax.fori_loop(0, groups, with_solve, 0)
    qg_copy = pltpu.make_async_copy(qg_s, qg_ref.at[0], out_sem.at[0])
    qg_copy.start()
    backward_z(2)
    weight_part(1)
    backward_y(3)
    backward_grads(2)
    scatter_near(1)
    backward_z(3)
    weight_part(2)
    reduce_two(0)
    backward_grads(3)
    scatter_near(2)
    weight_part(3)
    reduce_two(1)
    reduce_three(0)
    input_gradient()
    ig_copy = pltpu.make_async_copy(ig_s, ig_ref.at[0], out_sem.at[1])
    ig_copy.start()
    scatter_near(3)
    reduce_two(2)
    reduce_three(1)
    reduce_last(0)
    reduce_two(3)
    reduce_three(2)
    reduce_last(1)
    reduce_three(3)
    reduce_last(2)
    reduce_last(3)

    qg_copy.wait()
    ig_copy.wait()
    sent = pltpu.make_async_copy(
        fac_rcv.at[pl.ds(0, nctx - 1)], fac_rcv.at[pl.ds(0, nctx - 1)], fac_sem.at[0]
    )
    sent.wait()
    x_copy.wait_send()

    def drain(g, carry):
        wait_sent(snd1, g, s1)
        wait_sent(rcv1, g, s2)
        wait_sent(snd3, g, s3)
        wait_sent(rcv3, g, s4)
        sib_copy(g).wait_send()
        for part, (order, rws, lns, bufs) in enumerate(parts):
            for n in range(4):
                if count[order[max(n - 1, 0)]] > 1 and (n > 0 or count[order[0]] == 4):
                    wait_all(bufs[n].at[g], rs_snd.at[part, n, g])
        for back in range(2):
            for o in range(1, nz):
                to = lax.rem(mz + o, nz)

                @pl.when(to < mz if back else to > mz)
                def _():
                    total_copy(back, g, to).wait_send()

        return carry

    lax.fori_loop(0, groups, drain, 0)


def copy_kernel(a, b, c, d, a_out, b_out, c_out, d_out):
    for src, dst in ((a, a_out), (b, b_out), (c, c_out), (d, d_out)):
        dst[...] = src[...]


def copied(arrays):
    steps = 2
    specs = [
        pl.BlockSpec((1, a.shape[1] // steps, a.shape[2]), lambda i: (0, i, 0))
        if len(a.shape) == 3
        else pl.BlockSpec((a.shape[0] // steps, a.shape[1]), lambda i: (i, 0))
        for a in arrays
    ]
    return pl.pallas_call(
        copy_kernel,
        out_shape=tuple(jax.ShapeDtypeStruct(a.shape, a.dtype) for a in arrays),
        grid=(steps,),
        in_specs=specs,
        out_specs=tuple(specs),
        compiler_params=pltpu.CompilerParams(vmem_limit_bytes=62 << 20),
        name="results",
    )(*arrays)


def scatter_parts(rows):
    return (
        ("xyz", pl.ds(0, rows // 2), pl.ds(0, 3 * DK)),
        ("zxy", pl.ds(rows // 2, rows // 2), pl.ds(0, 3 * DK)),
        ("yzx", pl.ds(0, rows), pl.ds(3 * DK, DK)),
    )


def solution(mesh):
    nx = mesh.shape["dp"] // 2
    nctx = mesh.shape["ctx"]
    ny = min(nctx, 4)
    nz = nctx // ny

    def body(layer_input, queries, gates, regularizer, key_weight, value_weight, out_cotangent, lengths):
        tokens, width = layer_input.shape[1:]
        heads = gates.shape[2]
        groups = heads // PAIR
        rows = width // (2 * nx * nctx)
        tiles = PAIR * 24 // ny + 1
        wide = PAIR * 2 * DK
        state = lambda: pltpu.VMEM((groups, ny, tiles, 8, DK), F32)
        dma = lambda *shape: pltpu.SemaphoreType.DMA(shape)
        scratch = [
            pltpu.VMEM((tokens, width), BF16),
            pltpu.VMEM((heads, width, 2 * DK), BF16),
            pltpu.VMEM((heads, tokens, DK), BF16),
            pltpu.VMEM((heads, tokens, DK), BF16),
            pltpu.VMEM((tokens, width), BF16),
            pltpu.VMEM((tokens, heads * DK), F32),
            pltpu.VMEM((heads, tokens), F32),
            pltpu.VMEM((heads, tokens), F32),
            pltpu.VMEM((heads, tokens), F32),
            pltpu.VMEM((heads, tokens), F32),
            pltpu.VMEM((heads, DK), F32),
            pltpu.VMEM((nctx, heads, DK), F32),
            pltpu.VMEM((heads, 2, tokens, 2 * DK), BF16),
            pltpu.VMEM((heads, 2, DK, tokens), BF16),
            pltpu.VMEM((heads, tokens, tokens), F32),
            pltpu.VMEM((heads, tokens, tokens), F32),
            pltpu.VMEM((heads, DK, tokens), F32),
            pltpu.VMEM((heads, tokens, DK), F32),
            pltpu.VMEM((heads, tokens, 2 * DK), F32),
            state(), state(), state(), state(), state(), state(),
            pltpu.VMEM((2, groups, tiles, 8, DK), F32),
            pltpu.VMEM((2, groups, nz, tiles, 8, DK), F32),
            pltpu.VMEM((tiles, 8, DK), F32),
            pltpu.VMEM((tokens, width // 2), F32),
            pltpu.VMEM((tokens, width // 2), F32),
            pltpu.VMEM((width // 2, 2 * tokens), BF16),
            pltpu.VMEM((groups, 2 * tokens, wide), BF16),
            pltpu.VMEM((groups, tokens, wide), F32),
            pltpu.VMEM((groups, tokens, wide), F32),
        ]
        count = {"x": nx, "z": nz, "y": ny}
        for order, rws, lns in scatter_parts(rows):
            a, b, c = (count[axis] for axis in order)
            scratch.append(pltpu.VMEM((groups, a, b, c, rws.size, lns.size), F32))
            scratch.append(pltpu.VMEM((groups, 2, max(b // 2, 1), c, rws.size, lns.size), F32))
            for n in range(3):
                slots = 2 if n == 0 and count[order[0]] == 4 else max(count[order[n]] - 1, 1)
                left = tuple(count[a] for a in order[n + 1 :])
                scratch.append(pltpu.VMEM((groups, slots) + left + (rws.size, lns.size), F32))
        scratch += [dma(2), dma(3), dma(heads), dma(2), dma(2), dma(2, groups)]
        scratch += [dma(groups)] * 8 + [dma(2, groups, nz)] * 2 + [dma(3, 4, groups)] * 2
        any_space = pl.BlockSpec(memory_space=pl.ANY)
        vmem = pl.BlockSpec(memory_space=pltpu.VMEM)
        smem = pl.BlockSpec(memory_space=pltpu.SMEM)
        results = pl.pallas_call(
            functools.partial(mesa_kernel, (nx, nz, ny, heads, tokens, width)),
            out_shape=(
                jax.ShapeDtypeStruct((1, tokens, width), BF16),
                jax.ShapeDtypeStruct((1, tokens, heads * DK), F32),
                jax.ShapeDtypeStruct((rows, heads * DK), F32),
                jax.ShapeDtypeStruct((rows, heads * DK), F32),
            ),
            in_specs=[any_space, any_space, vmem, smem, any_space, any_space, any_space, smem],
            out_specs=(any_space, any_space, vmem, vmem),
            scratch_shapes=scratch,
            compiler_params=pltpu.CompilerParams(
                collective_id=0, has_side_effects=True, vmem_limit_bytes=63 << 20
            ),
            name="mesa_backward",
        )(layer_input, queries, jnp.swapaxes(gates, 1, 2), regularizer, key_weight, value_weight, out_cotangent, lengths)
        return copied(results)

    in_specs = (
        P("dp", "ctx", None),
        P("dp", "ctx", None),
        P("dp", "ctx", None),
        P(),
        P(),
        P(),
        P("dp", "ctx", None),
        P("dp", "ctx"),
    )
    out_specs = (
        P("dp", "ctx", None),
        P("dp", "ctx", None),
        P(("dp", "ctx"), None),
        P(("dp", "ctx"), None),
    )
    return jax.shard_map(body, mesh=mesh, in_specs=in_specs, out_specs=out_specs, check_vma=False)
```
